128 devices in a mesh: replica: 16 (over z_hi, x, core), fsdp: 8 (over y, z_lo).
Axes of the slice: x: 4, y: 4, z: 4 (z_hi: 2, z_lo: 2; z = z_hi * 2 + z_lo), core: 2. Of those that a mesh axis runs over, the one named last changes fastest.
Arguments:
- tokens: bfloat16 [16, 4096, 8192], P('replica', 'fsdp'), may hold values from -6 to 6
- targets: bfloat16 [16, 4096, 512], P('replica', 'fsdp'), may hold values from -6 to 6
- global_params: float32 [8192, 512], P('fsdp'), may hold values from -0.0625 to 0.0625
- drift: float32 [16, 8192, 512], P('replica', 'fsdp'), may hold values from -0.024 to 0.024
- first_moment: float32 [16, 8192, 512], P('replica', 'fsdp'), may hold values from -0.06 to 0.06
- second_moment: float32 [16, 8192, 512], P('replica', 'fsdp'), may hold values from 1e-05 to 0.001
- outer_momentum: float32 [8192, 512], P('fsdp'), may hold values from -0.03 to 0.03
Outputs:
- new_global: float32 [8192, 512], P('fsdp')
- new_momentum: float32 [8192, 512], P('fsdp')
The draws below stay inside these ranges and needn't reach their ends.
All inputs are finite; a program needn't handle non-finite values.
Results may differ from the reference program's by a relative error of at most 0.00049.
Values may be sent and summed in bfloat16 or wider, within the bound.
A program may use at most 128 MiB of HBM per device.

```python
import math
import jax
import jax.numpy as jnp
from jax import lax

D = 8192
KV = 512
TOKR = 4096
R = 16


def block_scale(rng, dims, split, low, high):
    def one(position, parts):
        draws = jax.random.uniform(jax.random.fold_in(jax.random.fold_in(rng, 6), position), (parts,), jnp.float32, low / len(split), high / len(split))
        return jnp.repeat(jnp.exp(draws), dims[position] // parts).reshape((-1,) + (1,) * (len(dims) - position - 1))

    loudness = one(*split[0])
    for cut in split[1:]:
        loudness = loudness * one(*cut)
    return loudness


def bell_draw(key, dims, width, limit, cuts=(), dtype=jnp.bfloat16):
    result = width * jax.random.normal(key, dims, jnp.float32)
    if cuts:
        result = result * block_scale(key, dims, cuts, -0.22, 0.18)
    return jnp.clip(result, -limit, limit).astype(dtype)


def setup_inputs(seed: int = 0) -> dict:
    key_list = jax.random.split(jax.random.key(seed), 8)
    return {
        "tokens": bell_draw(key_list[0], (R, TOKR, D), 1.0, 6.0, ((0, 16), (1, 8))),
        "targets": bell_draw(key_list[1], (R, TOKR, KV), 1.0, 6.0, ((0, 16), (1, 8))),
        "global_params": bell_draw(key_list[2], (D, KV), D ** -0.5, 0.0625, ((0, 8),), jnp.float32),
        "drift": bell_draw(key_list[3], (R, D, KV), 0.004, 0.024, ((0, 16), (1, 8)), jnp.float32),
        "first_moment": bell_draw(key_list[4], (R, D, KV), 0.01, 0.06, ((0, 16), (1, 8)), jnp.float32),
        "second_moment": jnp.clip(jnp.exp(math.log(0.001) - 4.6051703 * jax.random.uniform(key_list[5], (R, D, KV), jnp.float32) ** block_scale(key_list[5], (R, D, KV), ((0, 16), (1, 8)), -0.2, 0.2)), 9.999999747378752e-06, 0.001),
        "outer_momentum": bell_draw(key_list[6], (D, KV), 0.005, 0.03, ((0, 8),), jnp.float32),
    }


corr_one = 1.0 - 0.9 ** 20
corr_two = 1.0 - 0.95 ** 20

def replica_delta(global_params, tokens_r, targets_r, drift_r, moment_r, second_r):
    local = global_params + drift_r
    weight = local.astype(jnp.bfloat16)
    keys = jnp.dot(tokens_r, weight, preferred_element_type=jnp.float32)
    resid = (keys - targets_r.astype(jnp.float32)).astype(jnp.bfloat16)
    grad = lax.dot_general(tokens_r, resid, (((0,), (0,)), ((), ())), preferred_element_type=jnp.float32) / TOKR
    moment = 0.9 * moment_r + 0.1 * grad
    second = 0.95 * second_r + 0.05 * grad * grad
    update = moment / corr_one / (jnp.sqrt(second / corr_two) + 1e-08) + 0.1 * local
    local_new = local - 0.003 * update
    return global_params - local_new

def reference(tokens, targets, global_params, drift, first_moment, second_moment, outer_momentum):

    def one(carry, items):
        tokens_r, targets_r, drift_r, moment_r, second_r = items
        return (carry + replica_delta(global_params, tokens_r, targets_r, drift_r, moment_r, second_r), None)
    summed, _ = lax.scan(one, jnp.zeros((D, KV), jnp.float32), (tokens, targets, drift, first_moment, second_moment))
    average = summed / R
    new_momentum = 0.9 * outer_momentum + average
    new_global = global_params - 0.7 * (0.9 * new_momentum + average)
    return (new_global, new_momentum)
```

```python
import functools
import jax
import jax.numpy as jnp
from jax import lax
from jax.experimental import pallas as pl
from jax.experimental.pallas import tpu as pltpu
from jax.sharding import PartitionSpec as P

MESH = pl.DeviceIdType.MESH
F32 = jnp.float32
BF16 = jnp.bfloat16

corr_one = 1.0 - 0.9**20
corr_two = 1.0 - 0.95**20

TOK = 512
D = 8192
KV = 512
NS = 8
ROWS = D // NS
H = KV // 2
C = 4
R = ROWS // C
AP = (144, 112)
GP = (160, 96)
XR = R // 4
REPLICAS = 16


class Links:
    def __init__(self, send_sems, recv_sems):
        self.send_sems, self.recv_sems = send_sems, recv_sems
        self.index, self.sent = {}, []

    def _sems(self, name):
        i = self.index.setdefault(name, len(self.index))
        return self.send_sems.at[i], self.recv_sems.at[i]

    def send(self, name, src, dst, target):
        s, r = self._sems(name)
        copy = pltpu.make_async_remote_copy(
            src_ref=src, dst_ref=dst, send_sem=s, recv_sem=r, device_id=target, device_id_type=MESH
        )
        copy.start()
        self.sent.append(copy)

    def recv(self, name, dst, anyone):
        s, r = self._sems(name)
        pltpu.make_async_remote_copy(
            src_ref=dst, dst_ref=dst, send_sem=s, recv_sem=r, device_id=anyone, device_id_type=MESH
        ).wait_recv()

    def drain(self):
        for copy in self.sent:
            copy.wait_send()


N_MESSAGES = 192


def kernel(
    tok_hbm, tgt_hbm, gp_hbm, dr_hbm, m_hbm, v_hbm, out_hbm,
    tok, tokt, w, g, tgt, keys, resid, gp, dr, mo, ve,
    r_b1, r_b2, r_b3, r_b4, r_d1, r_d2, delta, r_c, r_x, r_z, avg,
    load_sem, part_sem, out_sem, send_sems, recv_sems,
):
    rep = lax.axis_index("replica")
    me = lax.axis_index("fsdp")
    zh, x, c = rep // 8, (rep // 2) % 4, rep % 2
    y, zl = me // 2, me % 2
    yp, ym, y2 = (y + 1) % 4, (y + 3) % 4, (y + 2) % 4
    oz = 1 - zl

    def shard(a, b):
        return a * 2 + b

    to_yp, to_ym = (rep, shard(yp, zl)), (rep, shard(ym, zl))
    to_z = (rep, shard(y, oz))
    to_c = (zh * 8 + x * 2 + (1 - c), me)
    to_x = [(zh * 8 + ((x + k) % 4) * 2 + c, me) for k in range(4)]
    to_zh = ((1 - zh) * 8 + x * 2 + c, me)
    friends = [to_yp, to_ym, to_z, to_c, to_x[1], to_x[2], to_x[3], to_zh]
    links = Links(send_sems, recv_sems)
    ydirs = ((0, to_yp, ym, yp), (1, to_ym, yp, ym))

    parts = []
    for k in range(C):
        rows = pl.ds(k * R, R)
        a = pltpu.make_async_copy(gp_hbm.at[rows], gp.at[rows], part_sem.at[0, k])
        b = pltpu.make_async_copy(dr_hbm.at[0, rows], dr.at[rows], part_sem.at[1, k])
        a.start()
        b.start()
        parts.append((a, b))
    load_tok = pltpu.make_async_copy(tok_hbm.at[0], tok, load_sem.at[0])
    load_tgt = pltpu.make_async_copy(tgt_hbm.at[0], tgt, load_sem.at[1])
    load_m = pltpu.make_async_copy(m_hbm.at[0], mo, load_sem.at[2])
    load_v = pltpu.make_async_copy(v_hbm.at[0], ve, load_sem.at[3])
    for copy in (load_tok, load_tgt, load_m, load_v):
        copy.start()

    barrier = pltpu.get_barrier_semaphore()
    for friend in friends:
        pl.semaphore_signal(barrier, inc=1, device_id=friend, device_id_type=MESH)

    def weights(k):
        for copy in parts[k]:
            copy.wait()
        rows = pl.ds(k * R, R)
        for h in range(2):
            cols = pl.ds(h * H, H)
            w[me, h, rows] = (gp[rows, cols] + dr[rows, cols]).astype(BF16)

    weights(0)
    pl.semaphore_wait(barrier, len(friends))

    def rows_of(k, part, split):
        if part is None:
            return pl.ds(k * R, R)
        return pl.ds(k * R + (split[0] if part else 0), split[part])

    def wpiece(s, k, part=None, h=None):
        rows = rows_of(k, part, AP)
        return w.at[s, :, rows] if h is None else w.at[s, h, rows]

    def wsend(name, piece, target):
        links.send(name, piece, piece, target)

    for k in range(C):
        if k:
            weights(k)
        for h, target, _, _ in ydirs:
            wsend(("a1", h, k), wpiece(me, k), target)
        wsend(("za", k), wpiece(me, k), to_z)

    load_tok.wait()

    def dot_keys(s, k):
        cols = pl.ds(pl.multiple_of(s * ROWS + k * R, R), R)
        for h in range(2):
            keys[h] += jnp.dot(tok[:, cols], w[s, h, pl.ds(k * R, R)], preferred_element_type=F32)

    own_cols = pl.ds(pl.multiple_of(me * ROWS, ROWS), ROWS)
    for h in range(2):
        keys[h] = jnp.dot(tok[:, own_cols], w[me, h], preferred_element_type=F32)

    @pl.loop(0, D // 256)
    def _(b):
        at = pl.ds(pl.multiple_of(b * 256, 256), 256)
        tokt[at, :] = tok[:, at].T

    for k in range(C):
        links.recv(("za", k), wpiece(shard(y, oz), k), to_z)
        for h, target, _, _ in ydirs:
            wsend(("a2", h, k), wpiece(shard(y, oz), k, 0), target)
        for h, target, src, _ in ydirs:
            links.recv(("a1", h, k), wpiece(shard(src, zl), k), target)
            wsend(("a3", h, k), wpiece(shard(src, zl), k, None, h), target)
            wsend(("z3", h, k), wpiece(shard(src, zl), k, 1), to_z)
        dot_keys(shard(y, oz), k)
        dot_keys(shard(ym, zl), k)
        dot_keys(shard(yp, zl), k)
    for k in range(C):
        for h, target, src, _ in ydirs:
            links.recv(("a3", h, k), wpiece(shard(y2, zl), k, None, h), target)
            wsend(("z5", h, k), wpiece(shard(y2, zl), k, 1, h), to_z)
        for h, target, src, _ in ydirs:
            links.recv(("a2", h, k), wpiece(shard(src, oz), k, 0), target)
            wsend(("a4", h, k), wpiece(shard(src, oz), k, 0, h), target)
        dot_keys(shard(y2, zl), k)
    for k in range(C):
        for h, target, src, _ in ydirs:
            links.recv(("z3", h, k), wpiece(shard(src, oz), k, 1), to_z)
            dot_keys(shard(src, oz), k)
        for h, target, src, _ in ydirs:
            links.recv(("z5", h, k), wpiece(shard(y2, oz), k, 1, h), to_z)
            links.recv(("a4", h, k), wpiece(shard(y2, oz), k, 0, h), target)
        dot_keys(shard(y2, oz), k)

    load_tgt.wait()
    for h in range(2):
        resid[h] = (keys[h] - tgt[:, pl.ds(h * H, H)].astype(F32)).astype(BF16)

    def grads(s, k):
        at = pl.ds(pl.multiple_of(s * ROWS + k * R, R), R)
        for h in range(2):
            g[s, h, pl.ds(k * R, R)] = jnp.dot(
                tokt[at, :], resid[h], preferred_element_type=F32
            ).astype(BF16)

    def gpiece(s, k, part, h=None):
        rows = rows_of(k, part, GP)
        return g.at[s, :, rows] if h is None else g.at[s, h, rows]

    def part_rows(k, part):
        return pl.ds(k * GP[part], GP[part])

    def s1(k):
        for z in range(2):
            grads(shard(y2, z), k)
        for h, target, _, _ in ydirs:
            for z in range(2):
                links.send(
                    ("b1", h, z, k), gpiece(shard(y2, z), k, 0, h), r_b1.at[h, z, part_rows(k, 0)], target
                )
        links.send(("d1", 2, k), gpiece(shard(y2, oz), k, 1), r_d1.at[2, :, part_rows(k, 1)], to_z)

        @pl.loop(0, 2)
        def _(z):
            for a in (yp, ym, y):
                grads(shard(a, z), k)

        for j, a in ((1, yp), (3, ym), (0, y)):
            links.send(("d1", j, k), gpiece(shard(a, oz), k, 1), r_d1.at[j, :, part_rows(k, 1)], to_z)

    def s2y(k):
        p = part_rows(k, 0)
        for h, target, _, dst in ydirs:
            for z in range(2):
                links.recv(("b1", h, z, k), r_b1.at[h, z, p], target)
                own = gpiece(shard(dst, z), k, 0, h)
                own[...] += r_b1[h, z, p]
                links.send(("b2", h, z, k), gpiece(shard(dst, z), k, 0), r_b2.at[h, z, :, p], target)

    def s2z(k):
        p = part_rows(k, 1)
        links.recv(("d1", 2, k), r_d1.at[2, :, p], to_z)
        own = gpiece(shard(y2, zl), k, 1)
        own[...] += r_d1[2, :, p]
        for h, target, _, _ in ydirs:
            links.send(("b3", h, k), gpiece(shard(y2, zl), k, 1, h), r_b3.at[h, p], target)

    def s3y(k):
        p = part_rows(k, 1)
        for h, target, _, dst in ydirs:
            j = 1 if h == 0 else 3
            links.recv(("d1", j, k), r_d1.at[j, :, p], to_z)
            links.recv(("b3", h, k), r_b3.at[h, p], target)
            one = gpiece(shard(dst, zl), k, 1, h)
            one[...] += r_d1[j, h, p] + r_b3[h, p]
            two = gpiece(shard(dst, zl), k, 1, 1 - h)
            two[...] += r_d1[j, 1 - h, p]
            links.send(("b4", h, k), gpiece(shard(dst, zl), k, 1), r_b4.at[h, :, p], target)

    def s3z(k):
        p = part_rows(k, 0)
        for h, target, _, _ in ydirs:
            for z in range(2):
                links.recv(("b2", h, z, k), r_b2.at[h, z, :, p], target)
        own = gpiece(shard(y, oz), k, 0)
        own[...] += r_b2[0, oz, :, p] + r_b2[1, oz, :, p]
        links.send(("d2", k), own, r_d2.at[:, p], to_z)

    def update(rows, cols, grad_sum):
        grad = grad_sum * (1.0 / (TOK * NS))
        glob = gp[rows, cols]
        local = glob + dr[rows, cols]
        moment = 0.9 * mo[rows, cols] + 0.1 * grad
        second = 0.95 * ve[rows, cols] + 0.05 * grad * grad
        step = moment / corr_one / (jnp.sqrt(second / corr_two) + 1e-08) + 0.1 * local
        return glob - (local - 0.003 * step)

    def s4(k):
        if k == 0:
            load_m.wait()
            load_v.wait()
        links.recv(("d2", k), r_d2.at[:, part_rows(k, 0)], to_z)
        sub = 32

        @pl.loop(0, GP[0] // sub)
        def _(i):
            off = pl.multiple_of(i * sub, sub)
            rows = pl.ds(k * R + off, sub)
            p = pl.ds(k * GP[0] + off, sub)
            for h in range(2):
                total = (
                    (g[me, h, rows].astype(F32) + r_d2[h, p].astype(F32))
                    + (r_b2[0, zl, h, p].astype(F32) + r_b2[1, zl, h, p].astype(F32))
                )
                delta[h, rows] = update(rows, pl.ds(h * H, H), total)

        links.recv(("d1", 0, k), r_d1.at[0, :, part_rows(k, 1)], to_z)
        for h, target, _, _ in ydirs:
            links.recv(("b4", h, k), r_b4.at[h, :, part_rows(k, 1)], target)

        @pl.loop(0, GP[1] // sub)
        def _(i):
            off = pl.multiple_of(i * sub, sub)
            rows = pl.ds(k * R + GP[0] + off, sub)
            p = pl.ds(k * GP[1] + off, sub)
            for h in range(2):
                total = (
                    (g[me, h, rows].astype(F32) + r_d1[0, h, p].astype(F32))
                    + (r_b4[0, h, p].astype(F32) + r_b4[1, h, p].astype(F32))
                )
                delta[h, rows] = update(rows, pl.ds(h * H, H), total)

        rows = pl.ds(k * R, R)
        links.send(("c", k), delta.at[1 - c, rows], r_c.at[rows], to_c)

    def x_rows(k, a):
        return pl.ds(pl.multiple_of(k * R + a * XR, XR), XR)

    def s5(k):
        rows = pl.ds(k * R, R)
        links.recv(("c", k), r_c.at[rows], to_c)
        delta[c, rows] += r_c[rows]
        for j in (2, 1, 3):
            links.send(
                ("x", j, k), delta.at[c, x_rows(k, (x + j) % 4)], r_x.at[j - 1, pl.ds(k * XR, XR)], to_x[j]
            )

    def s6(k):
        p = pl.ds(k * XR, XR)
        for j in (1, 3, 2):
            links.recv(("x", j, k), r_x.at[j - 1, p], to_x[j])
        at = x_rows(k, x)
        delta[c, at] += r_x[0, p] + r_x[1, p] + r_x[2, p]
        links.send(("zh", k), delta.at[c, at], r_z.at[p], to_zh)

    def s7(k):
        p = pl.ds(k * XR, XR)
        links.recv(("zh", k), r_z.at[p], to_zh)
        at = x_rows(k, x)
        avg[c, at] = (delta[c, at] + r_z[p]) * (1.0 / REPLICAS)
        for j in (2, 1, 3):
            links.send(("xg", j, k), avg.at[c, at], avg.at[c, at], to_x[j])

    out_copies = []

    def write_out(h, k):
        rows = pl.ds(k * R, R)
        cols = pl.ds(pl.multiple_of(h * H, H), H)
        copy = pltpu.make_async_copy(avg.at[h, rows], out_hbm.at[rows, cols], out_sem.at[len(out_copies)])
        copy.start()
        out_copies.append(copy)

    def s8(k):
        for j in (1, 3, 2):
            links.recv(("xg", j, k), avg.at[c, x_rows(k, (x + 4 - j) % 4)], to_x[j])
        rows = pl.ds(k * R, R)
        links.send(("cg", k), avg.at[c, rows], avg.at[c, rows], to_c)
        write_out(c, k)

    def s9(k):
        rows = pl.ds(k * R, R)
        links.recv(("cg", k), avg.at[1 - c, rows], to_c)
        write_out(1 - c, k)

    order = [
        (s1, 0), (s1, 1), (s2y, 0), (s2z, 0), (s1, 2), (s2y, 1), (s3z, 0), (s3y, 0), (s2z, 1), (s1, 3),
        (s2y, 2), (s4, 0), (s3z, 1), (s3y, 1), (s5, 0), (s2z, 2), (s2y, 3), (s6, 0), (s2z, 3), (s4, 1),
        (s7, 0), (s3z, 2), (s5, 1), (s3y, 2), (s8, 0), (s6, 1), (s3z, 3), (s3y, 3), (s4, 2), (s7, 1), (s9, 0), (s5, 2),
        (s8, 1), (s4, 3), (s6, 2), (s5, 3), (s7, 2), (s6, 3), (s9, 1), (s7, 3), (s8, 2), (s8, 3), (s9, 2), (s9, 3),
    ]
    for stage, k in order:
        stage(k)

    for copy in out_copies:
        copy.wait()
    links.drain()


def replica_average(tokens, targets, global_params, drift, first_moment, second_moment):
    any_space = pl.BlockSpec(memory_space=pl.ANY)
    p1, p2 = C * GP[0], C * GP[1]
    return pl.pallas_call(
        kernel,
        out_shape=jax.ShapeDtypeStruct((ROWS, KV), F32),
        in_specs=[any_space] * 6,
        out_specs=any_space,
        scratch_shapes=[
            pltpu.VMEM((TOK, D), BF16),
            pltpu.VMEM((D, TOK), BF16),
            pltpu.VMEM((NS, 2, ROWS, H), BF16),
            pltpu.VMEM((NS, 2, ROWS, H), BF16),
            pltpu.VMEM((TOK, KV), BF16),
            pltpu.VMEM((2, TOK, H), F32),
            pltpu.VMEM((2, TOK, H), BF16),
            pltpu.VMEM((ROWS, KV), F32),
            pltpu.VMEM((ROWS, KV), F32),
            pltpu.VMEM((ROWS, KV), F32),
            pltpu.VMEM((ROWS, KV), F32),
            pltpu.VMEM((2, 2, p1, H), BF16),
            pltpu.VMEM((2, 2, 2, p1, H), BF16),
            pltpu.VMEM((2, p2, H), BF16),
            pltpu.VMEM((2, 2, p2, H), BF16),
            pltpu.VMEM((4, 2, p2, H), BF16),
            pltpu.VMEM((2, p1, H), BF16),
            pltpu.VMEM((2, ROWS, H), F32),
            pltpu.VMEM((ROWS, H), F32),
            pltpu.VMEM((3, C * XR, H), F32),
            pltpu.VMEM((C * XR, H), F32),
            pltpu.VMEM((2, ROWS, H), F32),
            pltpu.SemaphoreType.DMA((4,)),
            pltpu.SemaphoreType.DMA((2, C)),
            pltpu.SemaphoreType.DMA((2 * C,)),
            pltpu.SemaphoreType.DMA((N_MESSAGES,)),
            pltpu.SemaphoreType.DMA((N_MESSAGES,)),
        ],
        compiler_params=pltpu.CompilerParams(
            collective_id=0, has_side_effects=True, vmem_limit_bytes=62 * 2**20
        ),
        cost_estimate=pl.CostEstimate(
            flops=4 * TOK * D * KV, bytes_accessed=24 * 2**20, transcendentals=ROWS * KV
        ),
        name="inner_step_and_average",
    )(tokens, targets, global_params, drift, first_moment, second_moment)


def shards(tokens, targets, global_params, drift, first_moment, second_moment, outer_momentum):
    average = replica_average(tokens, targets, global_params, drift, first_moment, second_moment)
    momentum_next = 0.9 * outer_momentum + average
    global_next = global_params - 0.7 * (0.9 * momentum_next + average)
    return (global_next, momentum_next)


def solution(mesh):
    in_specs = (
        P("replica", "fsdp", None),
        P("replica", "fsdp", None),
        P("fsdp", None),
        P("replica", "fsdp", None),
        P("replica", "fsdp", None),
        P("replica", "fsdp", None),
        P("fsdp", None),
    )
    out_specs = (P("fsdp", None), P("fsdp", None))
    return jax.shard_map(shards, mesh=mesh, in_specs=in_specs, out_specs=out_specs, check_vma=False)
```

```python
import functools
import jax
import jax.numpy as jnp
from jax import lax
from jax.experimental import pallas as pl
from jax.experimental.pallas import tpu as pltpu
from jax.sharding import PartitionSpec as P

MESH = pl.DeviceIdType.MESH
F32 = jnp.float32
BF16 = jnp.bfloat16

corr_one = 1.0 - 0.9**20
corr_two = 1.0 - 0.95**20

TOK = 512
D = 8192
KV = 512
NS = 8
ROWS = D // NS
H = KV // 2
C = 4
R = ROWS // C
AP = (144, 112)
GROUPS = ((144, 112), (160, 96), (144, 112), (64, 64), (48, 16), (32, 32))
N = len(GROUPS)
FAST = 1
SIZE = [sum(p) for p in GROUPS]
START = [sum(SIZE[:k]) for k in range(N)]
PSTART = [[sum(p[i] for p in GROUPS[:k]) for k in range(N)] for i in range(2)]
PROWS = [sum(p[i] for p in GROUPS) for i in range(2)]
REPLICAS = 16
VMEM_KIB = 50176


class Links:
    def __init__(self, send_sems, recv_sems):
        self.send_sems, self.recv_sems = send_sems, recv_sems
        self.index, self.sent = {}, []

    def _sems(self, name):
        i = self.index.setdefault(name, len(self.index))
        return self.send_sems.at[i], self.recv_sems.at[i]

    def send(self, name, src, dst, target):
        s, r = self._sems(name)
        copy = pltpu.make_async_remote_copy(
            src_ref=src, dst_ref=dst, send_sem=s, recv_sem=r, device_id=target, device_id_type=MESH
        )
        copy.start()
        self.sent.append(copy)

    def recv(self, name, dst, anyone):
        s, r = self._sems(name)
        pltpu.make_async_remote_copy(
            src_ref=dst, dst_ref=dst, send_sem=s, recv_sem=r, device_id=anyone, device_id_type=MESH
        ).wait_recv()

    def drain(self):
        for copy in self.sent:
            copy.wait_send()
        self.sent = []


N_MESSAGES = 208


def kernel(
    tok_hbm, tgt_hbm, gp_hbm, dr_hbm, m_hbm, v_hbm, om_hbm, new_global, new_momentum,
    tok, tokt, w, tgt, gp, dr, mo, ve, om,
    r_b1, r_b2, r_b3, r_b4, r_d1, r_d2, delta, r_c, r_x, r_z, r_f, avg,
    load_sem, part_sem, send_sems, recv_sems,
):
    rep = lax.axis_index("replica")
    me = lax.axis_index("fsdp")
    zh, x, c = rep // 8, (rep // 2) % 4, rep % 2
    y, zl = me // 2, me % 2
    yp, ym, y2 = (y + 1) % 4, (y + 3) % 4, (y + 2) % 4
    oz = 1 - zl

    def shard(a, b):
        return a * 2 + b

    to_yp, to_ym = (rep, shard(yp, zl)), (rep, shard(ym, zl))
    to_z = (rep, shard(y, oz))
    to_x = [(zh * 8 + ((x + k) % 4) * 2 + c, me) for k in range(4)]
    to_zh = ((1 - zh) * 8 + x * 2 + c, me)
    to_xc = [(zh * 8 + ((x + k) % 4) * 2 + (1 - c), me) for k in range(4)]
    friends = [to_yp, to_ym, to_z, to_zh] + to_x[1:] + to_xc
    links = Links(send_sems, recv_sems)
    ydirs = ((0, to_yp, ym, yp), (1, to_ym, yp, ym))

    parts = []
    for k in range(C):
        rows = pl.ds(k * R, R)
        a = pltpu.make_async_copy(gp_hbm.at[rows], gp.at[rows], part_sem.at[0, k])
        b = pltpu.make_async_copy(dr_hbm.at[0, rows], dr.at[rows], part_sem.at[1, k])
        a.start()
        b.start()
        parts.append((a, b))
    load_tok = pltpu.make_async_copy(tok_hbm.at[0], tok, load_sem.at[0])
    load_tgt = pltpu.make_async_copy(tgt_hbm.at[0], tgt, load_sem.at[1])
    load_m = pltpu.make_async_copy(m_hbm.at[0], mo, load_sem.at[2])
    load_v = pltpu.make_async_copy(v_hbm.at[0], ve, load_sem.at[3])
    load_om = pltpu.make_async_copy(om_hbm, om, load_sem.at[4])
    for copy in (load_tok, load_tgt, load_m, load_v, load_om):
        copy.start()

    barrier = pltpu.get_barrier_semaphore()
    for friend in friends:
        pl.semaphore_signal(barrier, inc=1, device_id=friend, device_id_type=MESH)

    def weights(k):
        for copy in parts[k]:
            copy.wait()
        rows = pl.ds(k * R, R)
        for h in range(2):
            cols = pl.ds(h * H, H)
            w[me, h, rows] = (gp[rows, cols] + dr[rows, cols]).astype(BF16)

    weights(0)
    pl.semaphore_wait(barrier, len(friends))

    def wpiece(s, k, part=None, h=None):
        rows = pl.ds(k * R, R) if part is None else pl.ds(k * R + (AP[0] if part else 0), AP[part])
        return w.at[s, :, rows] if h is None else w.at[s, h, rows]

    def wsend(name, piece, target):
        links.send(name, piece, piece, target)

    for k in range(C):
        if k:
            weights(k)
        for h, target, _, _ in ydirs:
            wsend(("a1", h, k), wpiece(me, k), target)
        wsend(("za", k), wpiece(me, k), to_z)

    load_tok.wait()
    keys = delta.at[:, pl.ds(0, TOK)]

    def dot_keys(s, k):
        cols = pl.ds(pl.multiple_of(s * ROWS + k * R, R), R)
        for h in range(2):
            keys[h] += jnp.dot(tok[:, cols], w[s, h, pl.ds(k * R, R)], preferred_element_type=F32)

    own_cols = pl.ds(pl.multiple_of(me * ROWS, ROWS), ROWS)
    for h in range(2):
        keys[h] = jnp.dot(tok[:, own_cols], w[me, h], preferred_element_type=F32)

    @pl.loop(0, D // 256)
    def _(b):
        at = pl.ds(pl.multiple_of(b * 256, 256), 256)
        tokt[at, :] = tok[:, at].T

    for k in range(C):
        links.recv(("za", k), wpiece(shard(y, oz), k), to_z)
        for h, target, _, _ in ydirs:
            wsend(("a2", h, k), wpiece(shard(y, oz), k, 0), target)
        for h, target, src, _ in ydirs:
            links.recv(("a1", h, k), wpiece(shard(src, zl), k), target)
            wsend(("a3", h, k), wpiece(shard(src, zl), k, None, h), target)
            wsend(("z3", h, k), wpiece(shard(src, zl), k, 1), to_z)
        dot_keys(shard(y, oz), k)
        dot_keys(shard(ym, zl), k)
        dot_keys(shard(yp, zl), k)
    for k in range(C):
        for h, target, src, _ in ydirs:
            links.recv(("a3", h, k), wpiece(shard(y2, zl), k, None, h), target)
            wsend(("z5", h, k), wpiece(shard(y2, zl), k, 1, h), to_z)
        for h, target, src, _ in ydirs:
            links.recv(("a2", h, k), wpiece(shard(src, oz), k, 0), target)
            wsend(("a4", h, k), wpiece(shard(src, oz), k, 0, h), target)
        dot_keys(shard(y2, zl), k)
    for k in range(C):
        for h, target, src, _ in ydirs:
            links.recv(("z3", h, k), wpiece(shard(src, oz), k, 1), to_z)
            dot_keys(shard(src, oz), k)
        for h, target, src, _ in ydirs:
            links.recv(("z5", h, k), wpiece(shard(y2, oz), k, 1, h), to_z)
            links.recv(("a4", h, k), wpiece(shard(y2, oz), k, 0, h), target)
        dot_keys(shard(y2, oz), k)

    load_tgt.wait()
    for h in range(2):
        cols = pl.ds(h * H, H)
        tgt[:, cols] = (keys[h] - tgt[:, cols].astype(F32)).astype(BF16)

    links.drain()
    g = w

    def grads(s, k):
        at = pl.ds(pl.multiple_of(s * ROWS + START[k], 16), SIZE[k])
        for h in range(2):
            g[s, h, pl.ds(START[k], SIZE[k])] = jnp.dot(
                tokt[at, :], tgt[:, pl.ds(h * H, H)], preferred_element_type=F32
            ).astype(BF16)

    def grows(k, part):
        return pl.ds(START[k] + (GROUPS[k][0] if part else 0), GROUPS[k][part])

    def gpiece(s, k, part, h=None):
        return g.at[s, :, grows(k, part)] if h is None else g.at[s, h, grows(k, part)]

    def gpair(a, k, h=None):
        two = pl.ds(pl.multiple_of(a * 2, 2), 2)
        return g.at[two, :, grows(k, 0)] if h is None else g.at[two, h, grows(k, 0)]

    def part_rows(k, part):
        return pl.ds(PSTART[part][k], GROUPS[k][part])

    def s1a(k):
        for z in range(2):
            grads(shard(y2, z), k)
        for h, target, _, _ in ydirs:
            links.send(("b1", h, k), gpair(y2, k, h), r_b1.at[h, :, part_rows(k, 0)], target)
        links.send(("d1", 2, k), gpiece(shard(y2, oz), k, 1), r_d1.at[2, :, part_rows(k, 1)], to_z)

    def s1b(k):
        @pl.loop(0, 2)
        def _(z):
            for a in (yp, ym, y):
                grads(shard(a, z), k)

        for j, a in ((1, yp), (3, ym), (0, y)):
            links.send(("d1", j, k), gpiece(shard(a, oz), k, 1), r_d1.at[j, :, part_rows(k, 1)], to_z)

    def s2y(h, k):
        p = part_rows(k, 0)
        _, target, _, dst = ydirs[h]
        links.recv(("b1", h, k), r_b1.at[h, :, p], target)
        own = gpair(dst, k, h)
        own[...] += r_b1[h, :, p]
        links.send(("b2", h, k), gpair(dst, k), r_b2.at[h, :, :, p], target)

    def s2z(k):
        p = part_rows(k, 1)
        links.recv(("d1", 2, k), r_d1.at[2, :, p], to_z)
        own = gpiece(shard(y2, zl), k, 1)
        own[...] += r_d1[2, :, p]
        for h, target, _, _ in ydirs:
            links.send(("b3", h, k), gpiece(shard(y2, zl), k, 1, h), r_b3.at[h, p], target)

    def s3y(h, k):
        p = part_rows(k, 1)
        _, target, _, dst = ydirs[h]
        j = 1 if h == 0 else 3
        links.recv(("d1", j, k), r_d1.at[j, :, p], to_z)
        links.recv(("b3", h, k), r_b3.at[h, p], target)
        one = gpiece(shard(dst, zl), k, 1, h)
        one[...] += r_d1[j, h, p] + r_b3[h, p]
        two = gpiece(shard(dst, zl), k, 1, 1 - h)
        two[...] += r_d1[j, 1 - h, p]
        links.send(("b4", h, k), gpiece(shard(dst, zl), k, 1), r_b4.at[h, :, p], target)

    def s3z(k):
        p = part_rows(k, 0)
        for h, target, _, _ in ydirs:
            links.recv(("b2", h, k), r_b2.at[h, :, :, p], target)
        own = gpiece(shard(y, oz), k, 0)
        own[...] += r_b2[0, oz, :, p] + r_b2[1, oz, :, p]
        links.send(("d2", k), own, r_d2.at[:, p], to_z)

    def update(rows, cols, grad_sum):
        grad = grad_sum * (1.0 / (TOK * NS))
        glob = gp[rows, cols]
        local = glob + dr[rows, cols]
        moment = 0.9 * mo[rows, cols] + 0.1 * grad
        second = 0.95 * ve[rows, cols] + 0.05 * grad * grad
        step = moment / corr_one / (jnp.sqrt(second / corr_two) + 1e-08) + 0.1 * local
        return glob - (local - 0.003 * step)

    def updates(k, part, total):
        sub = next(b for b in (48, 32, 16) if GROUPS[k][part] % b == 0)

        @pl.loop(0, GROUPS[k][part] // sub)
        def _(i):
            off = pl.multiple_of(i * sub, 16)
            rows = pl.ds(START[k] + (GROUPS[k][0] if part else 0) + off, sub)
            p = pl.ds(PSTART[part][k] + off, sub)
            for h in range(2):
                delta[h, rows] = update(rows, pl.ds(h * H, H), total(h, rows, p))

    def s4(k):
        if k == 0:
            load_m.wait()
            load_v.wait()
        links.recv(("d2", k), r_d2.at[:, part_rows(k, 0)], to_z)
        updates(
            k, 0,
            lambda h, rows, p: (g[me, h, rows].astype(F32) + r_d2[h, p].astype(F32))
            + (r_b2[0, zl, h, p].astype(F32) + r_b2[1, zl, h, p].astype(F32)),
        )
        links.recv(("d1", 0, k), r_d1.at[0, :, part_rows(k, 1)], to_z)
        for h, target, _, _ in ydirs:
            links.recv(("b4", h, k), r_b4.at[h, :, part_rows(k, 1)], target)
        updates(
            k, 1,
            lambda h, rows, p: (g[me, h, rows].astype(F32) + r_d1[0, h, p].astype(F32))
            + (r_b4[0, h, p].astype(F32) + r_b4[1, h, p].astype(F32)),
        )
        if k < N - FAST:
            rows = pl.ds(START[k], SIZE[k])
            links.send(("c", k), delta.at[1 - c, rows], r_c.at[rows], to_xc[0])
        else:
            for j, other, target in others():
                half = 1 - c if other else c
                links.send(
                    ("x", j, other, k), delta.at[half, x_rows(k, (x + j) % 4)], f_slot(j, other, k), target
                )

    def others():
        found = [(j, 0, to_x[j]) for j in (2, 1, 3)] + [(j, 1, to_xc[j]) for j in (2, 1, 3, 0)]
        return sorted(found, key=lambda f: (2, 1, 3, 0).index(f[0]))

    def x_rows(k, a):
        q = SIZE[k] // 4
        return pl.ds(pl.multiple_of(START[k] + a * q, 8), q)

    def q_rows(k):
        return pl.ds(START[k] // 4, SIZE[k] // 4)

    def f_slot(j, other, k):
        q = SIZE[k] // 4
        return r_f.at[j * 2 + other, pl.ds((START[k] - START[N - FAST]) // 4, q)]

    def s5(k):
        rows = pl.ds(START[k], SIZE[k])
        links.recv(("c", k), r_c.at[rows], to_xc[0])
        delta[c, rows] += r_c[rows]
        for j in (2, 1, 3):
            links.send(
                ("x", j, k), delta.at[c, x_rows(k, (x + j) % 4)], r_x.at[j - 1, q_rows(k)], to_x[j]
            )

    def s6(k):
        at = x_rows(k, x)
        if k < N - FAST:
            p = q_rows(k)
            for j in (1, 3, 2):
                links.recv(("x", j, k), r_x.at[j - 1, p], to_x[j])
            delta[c, at] += r_x[0, p] + r_x[1, p] + r_x[2, p]
        else:
            for j, other, target in reversed(others()):
                links.recv(("x", j, other, k), f_slot(j, other, k), target)
            total = delta[c, at]
            for j, other, _ in others():
                total += f_slot(j, other, k)[...]
            delta[c, at] = total
        links.send(("zh", k), delta.at[c, at], r_z.at[q_rows(k)], to_zh)

    def s7(k):
        links.recv(("zh", k), r_z.at[q_rows(k)], to_zh)
        at = x_rows(k, x)
        avg[c, at] = (delta[c, at] + r_z[q_rows(k)]) * (1.0 / REPLICAS)
        if k < N - FAST:
            for j in (2, 1, 3):
                links.send(("xg", j, k), avg.at[c, at], avg.at[c, at], to_x[j])
        else:
            for j, other, target in others():
                links.send(("xg", j, other, k), avg.at[c, at], avg.at[c, at], target)

    def outer(k, half):
        sub = 32

        @pl.loop(0, SIZE[k] // sub)
        def _(i):
            rows = pl.ds(START[k] + pl.multiple_of(i * sub, sub), sub)
            cols = pl.ds(pl.multiple_of(half * H, H), H)
            average = avg[half, rows]
            momentum_next = 0.9 * om[rows, cols] + average
            new_momentum[rows, cols] = momentum_next
            new_global[rows, cols] = gp[rows, cols] - 0.7 * (0.9 * momentum_next + average)

    def s8(k):
        for j in (1, 3, 2):
            links.recv(("xg", j, k), avg.at[c, x_rows(k, (x + 4 - j) % 4)], to_x[j])
        rows = pl.ds(START[k], SIZE[k])
        links.send(("cg", k), avg.at[c, rows], avg.at[c, rows], to_xc[0])
        if k == 0:
            load_om.wait()
        outer(k, c)

    def s9(k):
        if k < N - FAST:
            rows = pl.ds(START[k], SIZE[k])
            links.recv(("cg", k), avg.at[1 - c, rows], to_xc[0])
            outer(k, 1 - c)
        else:
            for j, other, target in reversed(others()):
                half = 1 - c if other else c
                links.recv(("xg", j, other, k), avg.at[half, x_rows(k, (x + 4 - j) % 4)], target)
            outer(k, 0)
            outer(k, 1)

    s2y0, s2y1 = functools.partial(s2y, 0), functools.partial(s2y, 1)
    s3y0, s3y1 = functools.partial(s3y, 0), functools.partial(s3y, 1)
    order = (
        (s1a, 3), (s1a, 0), (s1b, 0), (s1a, 1), (s2y1, 0), (s2y0, 0), (s1b, 1), (s2y1, 1), (s2y0, 1), (s2z, 0),
        (s2z, 1), (s1a, 2), (s3z, 0), (s3y1, 0), (s3y0, 0), (s1b, 3), (s2z, 2), (s3z, 1), (s1b, 2), (s3y1, 1),
        (s2z, 3), (s2y1, 2), (s3y0, 1), (s2y0, 2), (s4, 0), (s5, 0), (s2y0, 3), (s2y1, 3), (s4, 1), (s5, 1),
        (s6, 0), (s3y1, 2), (s3y0, 2), (s3z, 2), (s6, 1), (s1a, 4), (s1a, 5), (s3z, 3), (s7, 0), (s3y1, 3),
        (s1b, 4), (s3y0, 3), (s4, 2), (s2y0, 4), (s2y1, 4), (s7, 1), (s2z, 4), (s1b, 5), (s2z, 5), (s2y1, 5),
        (s8, 0), (s2y0, 5), (s5, 2), (s4, 3), (s8, 1), (s3z, 4), (s3y0, 4), (s3y1, 4), (s3y1, 5), (s3y0, 5),
        (s5, 3), (s3z, 5), (s6, 2), (s4, 4), (s4, 5), (s6, 3), (s5, 4), (s7, 2), (s6, 5), (s7, 3), (s6, 4),
        (s7, 4), (s8, 2), (s7, 5), (s9, 1), (s9, 0), (s8, 3), (s8, 4), (s9, 2), (s9, 5), (s9, 3), (s9, 4),
    )
    for stage, k in order:
        stage(k)
    links.drain()


def step(tokens, targets, global_params, drift, first_moment, second_moment, outer_momentum):
    in_hbm = pl.BlockSpec(memory_space=pltpu.HBM)
    in_vmem = pl.BlockSpec(memory_space=pltpu.VMEM)
    p1, p2 = PROWS
    return pl.pallas_call(
        kernel,
        out_shape=(jax.ShapeDtypeStruct((ROWS, KV), F32),) * 2,
        in_specs=[in_hbm] * 7,
        out_specs=(in_vmem, in_vmem),
        scratch_shapes=[
            pltpu.VMEM((TOK, D), BF16),
            pltpu.VMEM((D, TOK), BF16),
            pltpu.VMEM((NS, 2, ROWS, H), BF16),
            pltpu.VMEM((TOK, KV), BF16),
            pltpu.VMEM((ROWS, KV), F32),
            pltpu.VMEM((ROWS, KV), F32),
            pltpu.VMEM((ROWS, KV), F32),
            pltpu.VMEM((ROWS, KV), F32),
            pltpu.VMEM((ROWS, KV), F32),
            pltpu.VMEM((2, 2, p1, H), BF16),
            pltpu.VMEM((2, 2, 2, p1, H), BF16),
            pltpu.VMEM((2, p2, H), BF16),
            pltpu.VMEM((2, 2, p2, H), BF16),
            pltpu.VMEM((4, 2, p2, H), BF16),
            pltpu.VMEM((2, p1, H), BF16),
            pltpu.VMEM((2, ROWS, H), F32),
            pltpu.VMEM((ROWS, H), F32),
            pltpu.VMEM((3, ROWS // 4, H), F32),
            pltpu.VMEM((ROWS // 4, H), F32),
            pltpu.VMEM((8, sum(SIZE[N - FAST :]) // 4, H), F32),
            pltpu.VMEM((2, ROWS, H), F32),
            pltpu.SemaphoreType.DMA((5,)),
            pltpu.SemaphoreType.DMA((2, C)),
            pltpu.SemaphoreType.DMA((N_MESSAGES,)),
            pltpu.SemaphoreType.DMA((N_MESSAGES,)),
        ],
        compiler_params=pltpu.CompilerParams(
            collective_id=0, has_side_effects=True, vmem_limit_bytes=VMEM_KIB * 2**10
        ),
        cost_estimate=pl.CostEstimate(
            flops=4 * TOK * D * KV, bytes_accessed=24 * 2**20, transcendentals=ROWS * KV
        ),
        name="inner_and_outer_step",
    )(tokens, targets, global_params, drift, first_moment, second_moment, outer_momentum)


def solution(mesh):
    in_specs = (
        P("replica", "fsdp", None),
        P("replica", "fsdp", None),
        P("fsdp", None),
        P("replica", "fsdp", None),
        P("replica", "fsdp", None),
        P("replica", "fsdp", None),
        P("fsdp", None),
    )
    out_specs = (P("fsdp", None), P("fsdp", None))
    return jax.shard_map(step, mesh=mesh, in_specs=in_specs, out_specs=out_specs, check_vma=False)
```

```python
import functools
import jax
import jax.numpy as jnp
from jax import lax
from jax.experimental import pallas as pl
from jax.experimental.pallas import tpu as pltpu
from jax.sharding import PartitionSpec as P

MESH = pl.DeviceIdType.MESH
F32 = jnp.float32
BF16 = jnp.bfloat16

corr_one = 1.0 - 0.9**20
corr_two = 1.0 - 0.95**20

TOK = 512
D = 8192
KV = 512
NS = 8
ROWS = D // NS
H = KV // 2
C = 4
R = ROWS // C
AP = (144, 112)
GROUPS = ((144, 112), (160, 96), (144, 112), (64, 64), (48, 16), (32, 32))
N = len(GROUPS)
FAST = 1
SIZE = [sum(p) for p in GROUPS]
START = [sum(SIZE[:k]) for k in range(N)]
PSTART = [[sum(p[i] for p in GROUPS[:k]) for k in range(N)] for i in range(2)]
PROWS = [sum(p[i] for p in GROUPS) for i in range(2)]
REPLICAS = 16
VMEM_KIB = 50176


class Links:
    def __init__(self, send_sems, recv_sems):
        self.send_sems, self.recv_sems = send_sems, recv_sems
        self.index = {}

    def _sem(self, name):
        return self.recv_sems.at[self.index.setdefault(name, len(self.index))]

    def send(self, phase, name, src, dst, target):
        pltpu.make_async_remote_copy(
            src_ref=src, dst_ref=dst, send_sem=self.send_sems.at[phase], recv_sem=self._sem(name),
            device_id=target, device_id_type=MESH,
        ).start()

    def recv(self, name, like):
        pltpu.make_async_copy(like, like, self._sem(name)).wait()

    def sent(self, phase, like):
        pltpu.make_async_copy(like, like, self.send_sems.at[phase]).wait()


N_MESSAGES = 10 * C + 14 * N - 2 * FAST


def kernel(
    tok_hbm, tgt_hbm, gp_hbm, dr_hbm, m_hbm, v_hbm, om_hbm, new_global, new_momentum,
    tok, tokt, w, tgt, gp, dr, mo, ve, om,
    r_b1, r_b2, r_b3, r_b4, r_d1, r_d2, delta, r_c, r_x, r_z, r_f, avg,
    load_sem, part_sem, send_sems, recv_sems,
):
    rep = lax.axis_index("replica")
    me = lax.axis_index("fsdp")
    zh, x, c = rep // 8, (rep // 2) % 4, rep % 2
    y, zl = me // 2, me % 2
    yp, ym, y2 = (y + 1) % 4, (y + 3) % 4, (y + 2) % 4
    oz = 1 - zl

    def shard(a, b):
        return a * 2 + b

    to_yp, to_ym = (rep, shard(yp, zl)), (rep, shard(ym, zl))
    to_z = (rep, shard(y, oz))
    to_x = [(zh * 8 + ((x + k) % 4) * 2 + c, me) for k in range(4)]
    to_zh = ((1 - zh) * 8 + x * 2 + c, me)
    to_xc = [(zh * 8 + ((x + k) % 4) * 2 + (1 - c), me) for k in range(4)]
    friends = [to_yp, to_ym, to_z, to_zh] + to_x[1:] + to_xc
    links = Links(send_sems, recv_sems)
    ydirs = ((0, to_yp, ym, yp), (1, to_ym, yp, ym))

    parts = []
    for k in range(C):
        rows = pl.ds(k * R, R)
        a = pltpu.make_async_copy(gp_hbm.at[rows], gp.at[rows], part_sem.at[0, k])
        b = pltpu.make_async_copy(dr_hbm.at[0, rows], dr.at[rows], part_sem.at[1, k])
        a.start()
        b.start()
        parts.append((a, b))
    load_tok = pltpu.make_async_copy(tok_hbm.at[0], tok, load_sem.at[0])
    load_tgt = pltpu.make_async_copy(tgt_hbm.at[0], tgt, load_sem.at[1])
    load_m = pltpu.make_async_copy(m_hbm.at[0], mo, load_sem.at[2])
    load_v = pltpu.make_async_copy(v_hbm.at[0], ve, load_sem.at[3])
    load_om = pltpu.make_async_copy(om_hbm, om, load_sem.at[4])
    for copy in (load_tok, load_tgt, load_m, load_v, load_om):
        copy.start()

    barrier = pltpu.get_barrier_semaphore()
    for friend in friends:
        pl.semaphore_signal(barrier, inc=1, device_id=friend, device_id_type=MESH)

    def weights(k):
        for copy in parts[k]:
            copy.wait()
        rows = pl.ds(k * R, R)
        for h in range(2):
            cols = pl.ds(h * H, H)
            w[me, h, rows] = (gp[rows, cols] + dr[rows, cols]).astype(BF16)

    weights(0)
    pl.semaphore_wait(barrier, len(friends))

    def wpiece(s, k, part=None, h=None):
        rows = pl.ds(k * R, R) if part is None else pl.ds(k * R + (AP[0] if part else 0), AP[part])
        return w.at[s, :, rows] if h is None else w.at[s, h, rows]

    def wsend(name, piece, target):
        links.send(0, name, piece, piece, target)

    for k in range(C):
        if k:
            weights(k)
        for h, target, _, _ in ydirs:
            wsend(("a1", h, k), wpiece(me, k), target)
        wsend(("za", k), wpiece(me, k), to_z)

    load_tok.wait()
    keys = delta.at[:, pl.ds(0, TOK)]

    def dot_keys(s, k):
        cols = pl.ds(pl.multiple_of(s * ROWS + k * R, R), R)
        for h in range(2):
            keys[h] += jnp.dot(tok[:, cols], w[s, h, pl.ds(k * R, R)], preferred_element_type=F32)

    own_cols = pl.ds(pl.multiple_of(me * ROWS, ROWS), ROWS)
    for h in range(2):
        keys[h] = jnp.dot(tok[:, own_cols], w[me, h], preferred_element_type=F32)

    @pl.loop(0, D // 256)
    def _(b):
        at = pl.ds(pl.multiple_of(b * 256, 256), 256)
        tokt[at, :] = tok[:, at].T

    for k in range(C):
        links.recv(("za", k), wpiece(shard(y, oz), k))
        for h, target, _, _ in ydirs:
            wsend(("a2", h, k), wpiece(shard(y, oz), k, 0), target)
        for h, target, src, _ in ydirs:
            links.recv(("a1", h, k), wpiece(shard(src, zl), k))
            wsend(("a3", h, k), wpiece(shard(src, zl), k, None, h), target)
            wsend(("z3", k), wpiece(shard(src, zl), k, 1), to_z)
        dot_keys(shard(y, oz), k)
        dot_keys(shard(ym, zl), k)
        dot_keys(shard(yp, zl), k)
    for k in range(C):
        for h, target, src, _ in ydirs:
            links.recv(("a3", h, k), wpiece(shard(y2, zl), k, None, h))
            wsend(("z5", k), wpiece(shard(y2, zl), k, 1, h), to_z)
        for h, target, src, _ in ydirs:
            links.recv(("a2", h, k), wpiece(shard(src, oz), k, 0))
            wsend(("a4", k), wpiece(shard(src, oz), k, 0, h), target)
        dot_keys(shard(y2, zl), k)
    for k in range(C):
        links.recv(("z3", k), w.at[pl.ds(0, 2), :, pl.ds(0, AP[1])])
        dot_keys(shard(ym, oz), k)
        dot_keys(shard(yp, oz), k)
        links.recv(("z5", k), wpiece(shard(y2, oz), k, 1))
        links.recv(("a4", k), wpiece(shard(y2, oz), k, 0))
        dot_keys(shard(y2, oz), k)

    load_tgt.wait()
    for h in range(2):
        cols = pl.ds(h * H, H)
        tgt[:, cols] = (keys[h] - tgt[:, cols].astype(F32)).astype(BF16)

    links.sent(0, w.at[pl.ds(0, NS - 1)])
    g = w

    def grads(s, k):
        at = pl.ds(pl.multiple_of(s * ROWS + START[k], 16), SIZE[k])
        for h in range(2):
            g[s, h, pl.ds(START[k], SIZE[k])] = jnp.dot(
                tokt[at, :], tgt[:, pl.ds(h * H, H)], preferred_element_type=F32
            ).astype(BF16)

    def grows(k, part):
        return pl.ds(START[k] + (GROUPS[k][0] if part else 0), GROUPS[k][part])

    def gpiece(s, k, part, h=None):
        return g.at[s, :, grows(k, part)] if h is None else g.at[s, h, grows(k, part)]

    def gpair(a, k, h=None):
        two = pl.ds(pl.multiple_of(a * 2, 2), 2)
        return g.at[two, :, grows(k, 0)] if h is None else g.at[two, h, grows(k, 0)]

    def part_rows(k, part):
        return pl.ds(PSTART[part][k], GROUPS[k][part])

    def s1a(k):
        for z in range(2):
            grads(shard(y2, z), k)
        for h, target, _, _ in ydirs:
            links.send(1, ("b1", h, k), gpair(y2, k, h), r_b1.at[h, :, part_rows(k, 0)], target)
        links.send(1, ("da", k), gpiece(shard(y2, oz), k, 1), r_d1.at[3, :, part_rows(k, 1)], to_z)

    def s1b(k):
        @pl.loop(0, 2)
        def _(z):
            for a in (yp, ym, y):
                grads(shard(a, z), k)

        for j, a in ((0, yp), (1, ym), (2, y)):
            links.send(1, ("db", k), gpiece(shard(a, oz), k, 1), r_d1.at[j, :, part_rows(k, 1)], to_z)

    def s2y(h, k):
        p = part_rows(k, 0)
        _, target, _, dst = ydirs[h]
        links.recv(("b1", h, k), r_b1.at[h, :, p])
        own = gpair(dst, k, h)
        own[...] += r_b1[h, :, p]
        links.send(1, ("b2", k), gpair(dst, k), r_b2.at[h, :, :, p], target)

    def s2z(k):
        p = part_rows(k, 1)
        links.recv(("da", k), r_d1.at[3, :, p])
        own = gpiece(shard(y2, zl), k, 1)
        own[...] += r_d1[3, :, p]
        for h, target, _, _ in ydirs:
            links.send(1, ("b3", h, k), gpiece(shard(y2, zl), k, 1, h), r_b3.at[h, p], target)

    have_db = set()

    def s3y(h, k):
        p = part_rows(k, 1)
        _, target, _, dst = ydirs[h]
        if k not in have_db:
            have_db.add(k)
            links.recv(("db", k), r_d1.at[pl.ds(0, 3), :, p])
        links.recv(("b3", h, k), r_b3.at[h, p])
        one = gpiece(shard(dst, zl), k, 1, h)
        one[...] += r_d1[h, h, p] + r_b3[h, p]
        two = gpiece(shard(dst, zl), k, 1, 1 - h)
        two[...] += r_d1[h, 1 - h, p]
        links.send(1, ("b4", k), gpiece(shard(dst, zl), k, 1), r_b4.at[h, :, p], target)

    def s3z(k):
        p = part_rows(k, 0)
        links.recv(("b2", k), r_b2.at[:, :, :, p])
        own = gpiece(shard(y, oz), k, 0)
        own[...] += r_b2[0, oz, :, p] + r_b2[1, oz, :, p]
        links.send(1, ("d2", k), own, r_d2.at[:, p], to_z)

    def update(rows, cols, grad_sum):
        grad = grad_sum * (1.0 / (TOK * NS))
        glob = gp[rows, cols]
        local = glob + dr[rows, cols]
        moment = 0.9 * mo[rows, cols] + 0.1 * grad
        second = 0.95 * ve[rows, cols] + 0.05 * grad * grad
        step = moment / corr_one / (jnp.sqrt(second / corr_two) + 1e-08) + 0.1 * local
        return glob - (local - 0.003 * step)

    def updates(k, part, total):
        sub = next(b for b in (48, 32, 16) if GROUPS[k][part] % b == 0)

        @pl.loop(0, GROUPS[k][part] // sub)
        def _(i):
            off = pl.multiple_of(i * sub, 16)
            rows = pl.ds(START[k] + (GROUPS[k][0] if part else 0) + off, sub)
            p = pl.ds(PSTART[part][k] + off, sub)
            for h in range(2):
                delta[h, rows] = update(rows, pl.ds(h * H, H), total(h, rows, p))

    def s4(k):
        if k == 0:
            load_m.wait()
            load_v.wait()
        links.recv(("d2", k), r_d2.at[:, part_rows(k, 0)])
        updates(
            k, 0,
            lambda h, rows, p: (g[me, h, rows].astype(F32) + r_d2[h, p].astype(F32))
            + (r_b2[0, zl, h, p].astype(F32) + r_b2[1, zl, h, p].astype(F32)),
        )
        links.recv(("b4", k), r_b4.at[:, :, part_rows(k, 1)])
        updates(
            k, 1,
            lambda h, rows, p: (g[me, h, rows].astype(F32) + r_d1[2, h, p].astype(F32))
            + (r_b4[0, h, p].astype(F32) + r_b4[1, h, p].astype(F32)),
        )
        if k < N - FAST:
            rows = pl.ds(START[k], SIZE[k])
            links.send(2, ("c", k), delta.at[1 - c, rows], r_c.at[rows], to_xc[0])
        else:
            for j, other, target in others():
                half = 1 - c if other else c
                links.send(
                    2, ("x", k), delta.at[half, x_rows(k, (x + j) % 4)], f_slot(j, other, k), target
                )

    def others():
        found = [(j, 0, to_x[j]) for j in (2, 1, 3)] + [(j, 1, to_xc[j]) for j in (2, 1, 3, 0)]
        return sorted(found, key=lambda f: (2, 1, 3, 0).index(f[0]))

    def x_rows(k, a):
        q = SIZE[k] // 4
        return pl.ds(pl.multiple_of(START[k] + a * q, 8), q)

    def q_rows(k):
        return pl.ds(START[k] // 4, SIZE[k] // 4)

    def f_slot(j, other, k):
        q = SIZE[k] // 4
        return r_f.at[j * 2 + other, pl.ds((START[k] - START[N - FAST]) // 4, q)]

    def f_slots(k):
        q = SIZE[k] // 4
        return r_f.at[pl.ds(1, 7), pl.ds((START[k] - START[N - FAST]) // 4, q)]

    def s5(k):
        rows = pl.ds(START[k], SIZE[k])
        links.recv(("c", k), r_c.at[rows])
        delta[c, rows] += r_c[rows]
        for j in (2, 1, 3):
            links.send(
                2, ("x", k), delta.at[c, x_rows(k, (x + j) % 4)], r_x.at[j - 1, q_rows(k)], to_x[j]
            )

    def s6(k):
        at = x_rows(k, x)
        if k < N - FAST:
            p = q_rows(k)
            links.recv(("x", k), r_x.at[:, p])
            delta[c, at] += r_x[0, p] + r_x[1, p] + r_x[2, p]
        else:
            links.recv(("x", k), f_slots(k))
            total = delta[c, at]
            for j, other, _ in others():
                total += f_slot(j, other, k)[...]
            delta[c, at] = total
        links.send(2, ("zh", k), delta.at[c, at], r_z.at[q_rows(k)], to_zh)

    def s7(k):
        links.recv(("zh", k), r_z.at[q_rows(k)])
        at = x_rows(k, x)
        avg[c, at] = (delta[c, at] + r_z[q_rows(k)]) * (1.0 / REPLICAS)
        if k < N - FAST:
            for j in (2, 1, 3):
                links.send(2, ("xg", k), avg.at[c, at], avg.at[c, at], to_x[j])
        else:
            for j, other, target in others():
                links.send(2, ("xg", k), avg.at[c, at], avg.at[c, at], target)

    def outer(k, half):
        sub = 32

        @pl.loop(0, SIZE[k] // sub)
        def _(i):
            rows = pl.ds(START[k] + pl.multiple_of(i * sub, sub), sub)
            cols = pl.ds(pl.multiple_of(half * H, H), H)
            average = avg[half, rows]
            momentum_next = 0.9 * om[rows, cols] + average
            new_momentum[rows, cols] = momentum_next
            new_global[rows, cols] = gp[rows, cols] - 0.7 * (0.9 * momentum_next + average)

    def s8(k):
        links.recv(("xg", k), r_x.at[:, q_rows(k)])
        rows = pl.ds(START[k], SIZE[k])
        links.send(2, ("cg", k), avg.at[c, rows], avg.at[c, rows], to_xc[0])
        if k == 0:
            load_om.wait()
        outer(k, c)

    def s9(k):
        if k < N - FAST:
            rows = pl.ds(START[k], SIZE[k])
            links.recv(("cg", k), avg.at[1 - c, rows])
            outer(k, 1 - c)
        else:
            links.recv(("xg", k), f_slots(k))
            outer(k, 0)
            outer(k, 1)

    s2y0, s2y1 = functools.partial(s2y, 0), functools.partial(s2y, 1)
    s3y0, s3y1 = functools.partial(s3y, 0), functools.partial(s3y, 1)
    order = (
        (s1a, 3), (s1a, 0), (s1b, 0), (s1a, 1), (s1b, 1), (s2z, 0), (s1a, 2), (s2y1, 0), (s2y0, 0), (s3y1, 0),
        (s2z, 1), (s2y1, 1), (s3y0, 0), (s2y0, 1), (s3z, 0), (s3y0, 1), (s1b, 2), (s3y1, 1), (s2y1, 2),
        (s2y0, 2), (s2z, 3), (s4, 0), (s5, 0), (s3z, 1), (s1b, 3), (s2z, 2), (s2y1, 3), (s2y0, 3), (s6, 0),
        (s1a, 4), (s3z, 2), (s4, 1), (s3y0, 2), (s3y1, 2), (s5, 1), (s1a, 5), (s3y0, 3), (s3z, 3), (s3y1, 3),
        (s1b, 4), (s1b, 5), (s2y0, 4), (s2y1, 4), (s2z, 4), (s7, 0), (s4, 2), (s2z, 5), (s6, 1), (s2y0, 5),
        (s2y1, 5), (s4, 3), (s5, 2), (s3z, 4), (s3y0, 4), (s3y1, 4), (s5, 3), (s3y1, 5), (s8, 0), (s3z, 5),
        (s7, 1), (s3y0, 5), (s4, 4), (s6, 2), (s5, 4), (s4, 5), (s6, 3), (s7, 2), (s6, 4), (s8, 1), (s6, 5),
        (s7, 3), (s9, 0), (s7, 4), (s7, 5), (s8, 2), (s8, 3), (s9, 1), (s8, 4), (s9, 2), (s9, 3), (s9, 5),
        (s9, 4),
    )
    for stage, k in order:
        stage(k)
    links.sent(1, tokt.at[pl.ds(0, (NS - 1) * ROWS)])
    links.sent(2, tokt.at[pl.ds(0, 15 * ROWS // 4)])


def step(tokens, targets, global_params, drift, first_moment, second_moment, outer_momentum):
    in_hbm = pl.BlockSpec(memory_space=pltpu.HBM)
    in_vmem = pl.BlockSpec(memory_space=pltpu.VMEM)
    p1, p2 = PROWS
    return pl.pallas_call(
        kernel,
        out_shape=(jax.ShapeDtypeStruct((ROWS, KV), F32),) * 2,
        in_specs=[in_hbm] * 7,
        out_specs=(in_vmem, in_vmem),
        scratch_shapes=[
            pltpu.VMEM((TOK, D), BF16),
            pltpu.VMEM((D, TOK), BF16),
            pltpu.VMEM((NS, 2, ROWS, H), BF16),
            pltpu.VMEM((TOK, KV), BF16),
            pltpu.VMEM((ROWS, KV), F32),
            pltpu.VMEM((ROWS, KV), F32),
            pltpu.VMEM((ROWS, KV), F32),
            pltpu.VMEM((ROWS, KV), F32),
            pltpu.VMEM((ROWS, KV), F32),
            pltpu.VMEM((2, 2, p1, H), BF16),
            pltpu.VMEM((2, 2, 2, p1, H), BF16),
            pltpu.VMEM((2, p2, H), BF16),
            pltpu.VMEM((2, 2, p2, H), BF16),
            pltpu.VMEM((4, 2, p2, H), BF16),
            pltpu.VMEM((2, p1, H), BF16),
            pltpu.VMEM((2, ROWS, H), F32),
            pltpu.VMEM((ROWS, H), F32),
            pltpu.VMEM((3, ROWS // 4, H), F32),
            pltpu.VMEM((ROWS // 4, H), F32),
            pltpu.VMEM((8, sum(SIZE[N - FAST :]) // 4, H), F32),
            pltpu.VMEM((2, ROWS, H), F32),
            pltpu.SemaphoreType.DMA((5,)),
            pltpu.SemaphoreType.DMA((2, C)),
            pltpu.SemaphoreType.DMA((3,)),
            pltpu.SemaphoreType.DMA((N_MESSAGES,)),
        ],
        compiler_params=pltpu.CompilerParams(
            collective_id=0, has_side_effects=True, vmem_limit_bytes=VMEM_KIB * 2**10
        ),
        cost_estimate=pl.CostEstimate(
            flops=4 * TOK * D * KV, bytes_accessed=24 * 2**20, transcendentals=ROWS * KV
        ),
        name="inner_and_outer_step",
    )(tokens, targets, global_params, drift, first_moment, second_moment, outer_momentum)


def solution(mesh):
    in_specs = (
        P("replica", "fsdp", None),
        P("replica", "fsdp", None),
        P("fsdp", None),
        P("replica", "fsdp", None),
        P("replica", "fsdp", None),
        P("replica", "fsdp", None),
        P("fsdp", None),
    )
    out_specs = (P("fsdp", None), P("fsdp", None))
    return jax.shard_map(step, mesh=mesh, in_specs=in_specs, out_specs=out_specs, check_vma=False)
```

```python
import functools
import jax
import jax.numpy as jnp
from jax import lax
from jax.experimental import pallas as pl
from jax.experimental.pallas import tpu as pltpu
from jax.sharding import PartitionSpec as P

MESH = pl.DeviceIdType.MESH
F32 = jnp.float32
BF16 = jnp.bfloat16

corr_one = 1.0 - 0.9**20
corr_two = 1.0 - 0.95**20

TOK = 512
D = 8192
KV = 512
NS = 8
ROWS = D // NS
H = KV // 2
C = 4
R = ROWS // C
AP = (144, 112)
GROUPS = ((144, 112), (160, 96), (144, 112), (64, 64), (48, 16), (32, 32))
N = len(GROUPS)
FAST = 1
SIZE = [sum(p) for p in GROUPS]
START = [sum(SIZE[:k]) for k in range(N)]
PSTART = [[sum(p[i] for p in GROUPS[:k]) for k in range(N)] for i in range(2)]
PROWS = [sum(p[i] for p in GROUPS) for i in range(2)]
REPLICAS = 16
VMEM_KIB = 50176


class Links:
    def __init__(self, send_sems, recv_sems):
        self.send_sems, self.recv_sems = send_sems, recv_sems
        self.index = {}

    def _sem(self, name):
        return self.recv_sems.at[self.index.setdefault(name, len(self.index))]

    def send(self, phase, name, src, dst, target):
        pltpu.make_async_remote_copy(
            src_ref=src, dst_ref=dst, send_sem=self.send_sems.at[phase], recv_sem=self._sem(name),
            device_id=target, device_id_type=MESH,
        ).start()

    def recv(self, name, like):
        pltpu.make_async_copy(like, like, self._sem(name)).wait()

    def sent(self, phase, like):
        pltpu.make_async_copy(like, like, self.send_sems.at[phase]).wait()


N_MESSAGES = 10 * C + 14 * N - 2 * FAST


def kernel(
    tok_hbm, tgt_hbm, gp_hbm, dr_hbm, m_hbm, v_hbm, om_hbm, new_global, new_momentum,
    tok, tokt, w, tgt, gp, dr, mo, ve, om,
    r_b1, r_b2, r_b3, r_b4, r_d1, r_d2, delta, r_c, r_x, r_z, r_f, avg,
    load_sem, part_sem, send_sems, recv_sems,
):
    rep = lax.axis_index("replica")
    me = lax.axis_index("fsdp")
    zh, x, c = rep // 8, (rep // 2) % 4, rep % 2
    y, zl = me // 2, me % 2
    yp, ym, y2 = (y + 1) % 4, (y + 3) % 4, (y + 2) % 4
    oz = 1 - zl

    def shard(a, b):
        return a * 2 + b

    to_yp, to_ym = (rep, shard(yp, zl)), (rep, shard(ym, zl))
    to_z = (rep, shard(y, oz))
    to_x = [(zh * 8 + ((x + k) % 4) * 2 + c, me) for k in range(4)]
    to_zh = ((1 - zh) * 8 + x * 2 + c, me)
    to_xc = [(zh * 8 + ((x + k) % 4) * 2 + (1 - c), me) for k in range(4)]
    friends = [to_yp, to_ym, to_z, to_zh] + to_x[1:] + to_xc
    links = Links(send_sems, recv_sems)
    ydirs = ((0, to_yp, ym, yp), (1, to_ym, yp, ym))

    parts = []
    for k in range(C):
        rows = pl.ds(k * R, R)
        a = pltpu.make_async_copy(gp_hbm.at[rows], gp.at[rows], part_sem.at[0, k])
        b = pltpu.make_async_copy(dr_hbm.at[0, rows], dr.at[rows], part_sem.at[1, k])
        a.start()
        b.start()
        parts.append((a, b))
    load_tok = pltpu.make_async_copy(tok_hbm.at[0], tok, load_sem.at[0])
    load_tgt = pltpu.make_async_copy(tgt_hbm.at[0], tgt, load_sem.at[1])
    load_m = pltpu.make_async_copy(m_hbm.at[0], mo, load_sem.at[2])
    load_v = pltpu.make_async_copy(v_hbm.at[0], ve, load_sem.at[3])
    load_om = pltpu.make_async_copy(om_hbm, om, load_sem.at[4])
    for copy in (load_tok, load_tgt, load_m, load_v, load_om):
        copy.start()

    barrier = pltpu.get_barrier_semaphore()
    for friend in friends:
        pl.semaphore_signal(barrier, inc=1, device_id=friend, device_id_type=MESH)

    def weights(k):
        for copy in parts[k]:
            copy.wait()
        rows = pl.ds(k * R, R)
        for h in range(2):
            cols = pl.ds(h * H, H)
            w[me, h, rows] = (gp[rows, cols] + dr[rows, cols]).astype(BF16)

    weights(0)
    pl.semaphore_wait(barrier, len(friends))

    def wpiece(s, k, part=None, h=None):
        rows = pl.ds(k * R, R) if part is None else pl.ds(k * R + (AP[0] if part else 0), AP[part])
        return w.at[s, :, rows] if h is None else w.at[s, h, rows]

    def wsend(name, piece, target):
        links.send(0, name, piece, piece, target)

    for k in range(C):
        if k:
            weights(k)
        for h, target, _, _ in ydirs:
            wsend(("a1", h, k), wpiece(me, k), target)
        wsend(("za", k), wpiece(me, k), to_z)

    load_tok.wait()
    keys = delta.at[:, pl.ds(0, TOK)]

    def dot_keys(s, k):
        cols = pl.ds(pl.multiple_of(s * ROWS + k * R, R), R)
        for h in range(2):
            keys[h] += jnp.dot(tok[:, cols], w[s, h, pl.ds(k * R, R)], preferred_element_type=F32)

    own_cols = pl.ds(pl.multiple_of(me * ROWS, ROWS), ROWS)
    for h in range(2):
        keys[h] = jnp.dot(tok[:, own_cols], w[me, h], preferred_element_type=F32)

    @pl.loop(0, D // 256)
    def _(b):
        at = pl.ds(pl.multiple_of(b * 256, 256), 256)
        tokt[at, :] = tok[:, at].T

    for k in range(C):
        links.recv(("za", k), wpiece(shard(y, oz), k))
        for h, target, _, _ in ydirs:
            wsend(("a2", h, k), wpiece(shard(y, oz), k, 0), target)
        for h, target, src, _ in ydirs:
            links.recv(("a1", h, k), wpiece(shard(src, zl), k))
            wsend(("a3", h, k), wpiece(shard(src, zl), k, None, h), target)
            wsend(("z3", k), wpiece(shard(src, zl), k, 1), to_z)
        dot_keys(shard(y, oz), k)
        dot_keys(shard(ym, zl), k)
        dot_keys(shard(yp, zl), k)
    for k in range(C):
        for h, target, src, _ in ydirs:
            links.recv(("a3", h, k), wpiece(shard(y2, zl), k, None, h))
            wsend(("z5", k), wpiece(shard(y2, zl), k, 1, h), to_z)
        for h, target, src, _ in ydirs:
            links.recv(("a2", h, k), wpiece(shard(src, oz), k, 0))
            wsend(("a4", k), wpiece(shard(src, oz), k, 0, h), target)
        dot_keys(shard(y2, zl), k)
    for k in range(C):
        links.recv(("z3", k), w.at[pl.ds(0, 2), :, pl.ds(0, AP[1])])
        dot_keys(shard(ym, oz), k)
        dot_keys(shard(yp, oz), k)
        links.recv(("z5", k), wpiece(shard(y2, oz), k, 1))
        links.recv(("a4", k), wpiece(shard(y2, oz), k, 0))
        dot_keys(shard(y2, oz), k)

    load_tgt.wait()
    for h in range(2):
        cols = pl.ds(h * H, H)
        tgt[:, cols] = (keys[h] - tgt[:, cols].astype(F32)).astype(BF16)

    links.sent(0, w.at[pl.ds(0, NS - 1)])
    g = w

    def grads(s, k):
        at = pl.ds(pl.multiple_of(s * ROWS + START[k], 16), SIZE[k])
        for h in range(2):
            g[s, h, pl.ds(START[k], SIZE[k])] = jnp.dot(
                tokt[at, :], tgt[:, pl.ds(h * H, H)], preferred_element_type=F32
            ).astype(BF16)

    def grows(k, part):
        return pl.ds(START[k] + (GROUPS[k][0] if part else 0), GROUPS[k][part])

    def gpiece(s, k, part, h=None):
        return g.at[s, :, grows(k, part)] if h is None else g.at[s, h, grows(k, part)]

    def gpair(a, k, h=None):
        two = pl.ds(pl.multiple_of(a * 2, 2), 2)
        return g.at[two, :, grows(k, 0)] if h is None else g.at[two, h, grows(k, 0)]

    def part_rows(k, part):
        return pl.ds(PSTART[part][k], GROUPS[k][part])

    def s1a(k):
        for z in range(2):
            grads(shard(y2, z), k)
        for h, target, _, _ in ydirs:
            links.send(1, ("b1", h, k), gpair(y2, k, h), r_b1.at[h, :, part_rows(k, 0)], target)
        links.send(1, ("da", k), gpiece(shard(y2, oz), k, 1), r_d1.at[3, :, part_rows(k, 1)], to_z)

    def s1b(k):
        @pl.loop(0, 2)
        def _(z):
            for a in (yp, ym, y):
                grads(shard(a, z), k)

        for j, a in ((0, yp), (1, ym), (2, y)):
            links.send(1, ("db", k), gpiece(shard(a, oz), k, 1), r_d1.at[j, :, part_rows(k, 1)], to_z)

    def s2y(h, k):
        p = part_rows(k, 0)
        _, target, _, dst = ydirs[h]
        links.recv(("b1", h, k), r_b1.at[h, :, p])
        own = gpair(dst, k, h)
        own[...] += r_b1[h, :, p]
        links.send(1, ("b2", k), gpair(dst, k), r_b2.at[h, :, :, p], target)

    def s2z(k):
        p = part_rows(k, 1)
        links.recv(("da", k), r_d1.at[3, :, p])
        own = gpiece(shard(y2, zl), k, 1)
        own[...] += r_d1[3, :, p]
        for h, target, _, _ in ydirs:
            links.send(1, ("b3", h, k), gpiece(shard(y2, zl), k, 1, h), r_b3.at[h, p], target)

    have_db = set()

    def s3y(h, k):
        p = part_rows(k, 1)
        _, target, _, dst = ydirs[h]
        if k not in have_db:
            have_db.add(k)
            links.recv(("db", k), r_d1.at[pl.ds(0, 3), :, p])
        links.recv(("b3", h, k), r_b3.at[h, p])
        one = gpiece(shard(dst, zl), k, 1, h)
        one[...] += r_d1[h, h, p] + r_b3[h, p]
        two = gpiece(shard(dst, zl), k, 1, 1 - h)
        two[...] += r_d1[h, 1 - h, p]
        links.send(1, ("b4", k), gpiece(shard(dst, zl), k, 1), r_b4.at[h, :, p], target)

    def s3z(k):
        p = part_rows(k, 0)
        links.recv(("b2", k), r_b2.at[:, :, :, p])
        own = gpiece(shard(y, oz), k, 0)
        own[...] += r_b2[0, oz, :, p] + r_b2[1, oz, :, p]
        links.send(1, ("d2", k), own, r_d2.at[:, p], to_z)

    def update(rows, cols, grad_sum):
        grad = grad_sum * (1.0 / (TOK * NS))
        glob = gp[rows, cols]
        local = glob + dr[rows, cols]
        moment = 0.9 * mo[rows, cols] + 0.1 * grad
        second = 0.95 * ve[rows, cols] + 0.05 * grad * grad
        step = moment / corr_one / (jnp.sqrt(second / corr_two) + 1e-08) + 0.1 * local
        return glob - (local - 0.003 * step)

    def updates(k, part, total):
        sub = next(b for b in (48, 32, 16) if GROUPS[k][part] % b == 0)

        @pl.loop(0, GROUPS[k][part] // sub)
        def _(i):
            off = pl.multiple_of(i * sub, 16)
            rows = pl.ds(START[k] + (GROUPS[k][0] if part else 0) + off, sub)
            p = pl.ds(PSTART[part][k] + off, sub)
            for h in range(2):
                delta[h, rows] = update(rows, pl.ds(h * H, H), total(h, rows, p))

    def s4(k):
        if k == 0:
            load_m.wait()
            load_v.wait()
        links.recv(("d2", k), r_d2.at[:, part_rows(k, 0)])
        updates(
            k, 0,
            lambda h, rows, p: (g[me, h, rows].astype(F32) + r_d2[h, p].astype(F32))
            + (r_b2[0, zl, h, p].astype(F32) + r_b2[1, zl, h, p].astype(F32)),
        )
        links.recv(("b4", k), r_b4.at[:, :, part_rows(k, 1)])
        updates(
            k, 1,
            lambda h, rows, p: (g[me, h, rows].astype(F32) + r_d1[2, h, p].astype(F32))
            + (r_b4[0, h, p].astype(F32) + r_b4[1, h, p].astype(F32)),
        )
        if k < N - FAST:
            rows = pl.ds(START[k], SIZE[k])
            links.send(2, ("c", k), delta.at[1 - c, rows], r_c.at[rows], to_xc[0])
        else:
            for j, other, target in others():
                half = 1 - c if other else c
                links.send(
                    2, ("x", k), delta.at[half, x_rows(k, (x + j) % 4)], f_slot(j, other, k), target
                )

    def others():
        found = [(j, 0, to_x[j]) for j in (2, 1, 3)] + [(j, 1, to_xc[j]) for j in (2, 1, 3, 0)]
        return sorted(found, key=lambda f: (2, 1, 3, 0).index(f[0]))

    def x_rows(k, a):
        q = SIZE[k] // 4
        return pl.ds(pl.multiple_of(START[k] + a * q, 8), q)

    def q_rows(k):
        return pl.ds(START[k] // 4, SIZE[k] // 4)

    def f_slot(j, other, k):
        q = SIZE[k] // 4
        return r_f.at[j * 2 + other, pl.ds((START[k] - START[N - FAST]) // 4, q)]

    def f_slots(k):
        q = SIZE[k] // 4
        return r_f.at[pl.ds(1, 7), pl.ds((START[k] - START[N - FAST]) // 4, q)]

    def s5(k):
        rows = pl.ds(START[k], SIZE[k])
        links.recv(("c", k), r_c.at[rows])
        delta[c, rows] += r_c[rows]
        for j in (2, 1, 3):
            links.send(
                2, ("x", k), delta.at[c, x_rows(k, (x + j) % 4)], r_x.at[j - 1, q_rows(k)], to_x[j]
            )

    def s6(k):
        at = x_rows(k, x)
        if k < N - FAST:
            p = q_rows(k)
            links.recv(("x", k), r_x.at[:, p])
            delta[c, at] += r_x[0, p] + r_x[1, p] + r_x[2, p]
        else:
            links.recv(("x", k), f_slots(k))
            total = delta[c, at]
            for j, other, _ in others():
                total += f_slot(j, other, k)[...]
            delta[c, at] = total
        links.send(2, ("zh", k), delta.at[c, at], r_z.at[q_rows(k)], to_zh)

    def s7(k):
        links.recv(("zh", k), r_z.at[q_rows(k)])
        at = x_rows(k, x)
        avg[c, at] = (delta[c, at] + r_z[q_rows(k)]) * (1.0 / REPLICAS)
        if k < N - FAST:
            for j in (2, 1, 3):
                links.send(2, ("xg", k), avg.at[c, at], avg.at[c, at], to_x[j])
        else:
            for j, other, target in others():
                links.send(2, ("xg", k), avg.at[c, at], avg.at[c, at], target)

    def outer(k, half):
        sub = 32

        @pl.loop(0, SIZE[k] // sub)
        def _(i):
            rows = pl.ds(START[k] + pl.multiple_of(i * sub, sub), sub)
            cols = pl.ds(pl.multiple_of(half * H, H), H)
            average = avg[half, rows]
            momentum_next = 0.9 * om[rows, cols] + average
            new_momentum[rows, cols] = momentum_next
            new_global[rows, cols] = gp[rows, cols] - 0.7 * (0.9 * momentum_next + average)

    def s8(k):
        links.recv(("xg", k), r_x.at[:, q_rows(k)])
        rows = pl.ds(START[k], SIZE[k])
        links.send(2, ("cg", k), avg.at[c, rows], avg.at[c, rows], to_xc[0])
        if k == 0:
            load_om.wait()
        outer(k, c)

    def s9(k):
        if k < N - FAST:
            rows = pl.ds(START[k], SIZE[k])
            links.recv(("cg", k), avg.at[1 - c, rows])
            outer(k, 1 - c)
        else:
            links.recv(("xg", k), f_slots(k))
            outer(k, 0)
            outer(k, 1)

    s2y0, s2y1 = functools.partial(s2y, 0), functools.partial(s2y, 1)
    s3y0, s3y1 = functools.partial(s3y, 0), functools.partial(s3y, 1)
    order = (
        (s1a, 3), (s1a, 0), (s1b, 0), (s1a, 1), (s1b, 1), (s2z, 0), (s1a, 2), (s2y1, 0), (s2y0, 0), (s3y1, 0),
        (s2z, 1), (s2y1, 1), (s3y0, 0), (s2y0, 1), (s3z, 0), (s3y0, 1), (s1b, 2), (s3y1, 1), (s2y1, 2),
        (s2y0, 2), (s2z, 3), (s4, 0), (s5, 0), (s3z, 1), (s1b, 3), (s2z, 2), (s2y1, 3), (s2y0, 3), (s6, 0),
        (s1a, 4), (s3z, 2), (s4, 1), (s3y0, 2), (s3y1, 2), (s5, 1), (s1a, 5), (s3y0, 3), (s3z, 3), (s3y1, 3),
        (s1b, 4), (s1b, 5), (s2y0, 4), (s2y1, 4), (s2z, 4), (s7, 0), (s4, 2), (s2z, 5), (s6, 1), (s2y0, 5),
        (s2y1, 5), (s4, 3), (s5, 2), (s3z, 4), (s3y0, 4), (s3y1, 4), (s5, 3), (s3y1, 5), (s8, 0), (s3z, 5),
        (s7, 1), (s3y0, 5), (s4, 4), (s6, 2), (s5, 4), (s4, 5), (s6, 3), (s7, 2), (s6, 4), (s8, 1), (s6, 5),
        (s7, 3), (s9, 0), (s7, 4), (s7, 5), (s8, 2), (s8, 3), (s9, 1), (s8, 4), (s9, 2), (s9, 3), (s9, 5),
        (s9, 4),
    )
    for stage, k in order:
        stage(k)
    links.sent(1, tokt.at[pl.ds(0, (NS - 1) * ROWS)])
    links.sent(2, tokt.at[pl.ds(0, 15 * ROWS // 4)])


def step(*arrays):
    in_hbm = pl.BlockSpec(memory_space=pltpu.HBM)
    in_vmem = pl.BlockSpec(memory_space=pltpu.VMEM)
    p1, p2 = PROWS
    return pl.pallas_call(
        kernel,
        out_shape=(jax.ShapeDtypeStruct((ROWS, KV), F32),) * 2,
        in_specs=[in_hbm] * 7,
        out_specs=(in_vmem, in_vmem),
        scratch_shapes=[
            pltpu.VMEM((TOK, D), BF16),
            pltpu.VMEM((D, TOK), BF16),
            pltpu.VMEM((NS, 2, ROWS, H), BF16),
            pltpu.VMEM((TOK, KV), BF16),
            pltpu.VMEM((ROWS, KV), F32),
            pltpu.VMEM((ROWS, KV), F32),
            pltpu.VMEM((ROWS, KV), F32),
            pltpu.VMEM((ROWS, KV), F32),
            pltpu.VMEM((ROWS, KV), F32),
            pltpu.VMEM((2, 2, p1, H), BF16),
            pltpu.VMEM((2, 2, 2, p1, H), BF16),
            pltpu.VMEM((2, p2, H), BF16),
            pltpu.VMEM((2, 2, p2, H), BF16),
            pltpu.VMEM((4, 2, p2, H), BF16),
            pltpu.VMEM((2, p1, H), BF16),
            pltpu.VMEM((2, ROWS, H), F32),
            pltpu.VMEM((ROWS, H), F32),
            pltpu.VMEM((3, ROWS // 4, H), F32),
            pltpu.VMEM((ROWS // 4, H), F32),
            pltpu.VMEM((8, sum(SIZE[N - FAST :]) // 4, H), F32),
            pltpu.VMEM((2, ROWS, H), F32),
            pltpu.SemaphoreType.DMA((5,)),
            pltpu.SemaphoreType.DMA((2, C)),
            pltpu.SemaphoreType.DMA((3,)),
            pltpu.SemaphoreType.DMA((N_MESSAGES,)),
        ],
        compiler_params=pltpu.CompilerParams(
            collective_id=0, has_side_effects=True, vmem_limit_bytes=VMEM_KIB * 2**10
        ),
        cost_estimate=pl.CostEstimate(
            flops=4 * TOK * D * KV, bytes_accessed=24 * 2**20, transcendentals=ROWS * KV
        ),
        name="inner_and_outer_step",
    )(*(pltpu.with_memory_space_constraint(a, pltpu.HBM) for a in arrays))


def write_kernel(a_ref, b_ref, a_hbm, b_hbm, sems):
    copies = []
    for i, (src, dst) in enumerate(((a_ref, a_hbm), (b_ref, b_hbm))):
        for q in range(2):
            rows = pl.ds(q * ROWS // 2, ROWS // 2)
            copies.append(pltpu.make_async_copy(src.at[rows], dst.at[rows], sems.at[i, q]))
    for copy in copies:
        copy.start()
    for copy in copies:
        copy.wait()


def whole(*arrays):
    return pl.pallas_call(
        write_kernel,
        out_shape=(jax.ShapeDtypeStruct((ROWS, KV), F32),) * 2,
        in_specs=[pl.BlockSpec(memory_space=pl.ANY)] * 2,
        out_specs=(pl.BlockSpec(memory_space=pltpu.HBM),) * 2,
        scratch_shapes=[pltpu.SemaphoreType.DMA((2, 2))],
        compiler_params=pltpu.CompilerParams(vmem_limit_bytes=2**20),
        name="write_results",
    )(*step(*arrays))


def solution(mesh):
    in_specs = (
        P("replica", "fsdp", None),
        P("replica", "fsdp", None),
        P("fsdp", None),
        P("replica", "fsdp", None),
        P("replica", "fsdp", None),
        P("replica", "fsdp", None),
        P("fsdp", None),
    )
    out_specs = (P("fsdp", None), P("fsdp", None))
    return jax.shard_map(whole, mesh=mesh, in_specs=in_specs, out_specs=out_specs, check_vma=False)
```

```python
import functools
import jax
import jax.numpy as jnp
from jax import lax
from jax.experimental import pallas as pl
from jax.experimental.pallas import tpu as pltpu
from jax.sharding import PartitionSpec as P

MESH = pl.DeviceIdType.MESH
F32 = jnp.float32
BF16 = jnp.bfloat16

corr_one = 1.0 - 0.9**20
corr_two = 1.0 - 0.95**20

TOK = 512
D = 8192
KV = 512
NS = 8
ROWS = D // NS
H = KV // 2
C = 4
R = ROWS // C
AP = (144, 112)
GROUPS = ((160, 96), (144, 112), (112, 80), (112, 80), (32, 32), (32, 32))
N = len(GROUPS)
FAST = 1
SIZE = [sum(p) for p in GROUPS]
START = [sum(SIZE[:k]) for k in range(N)]
PSTART = [[sum(p[i] for p in GROUPS[:k]) for k in range(N)] for i in range(2)]
PROWS = [sum(p[i] for p in GROUPS) for i in range(2)]
WIDE = 2
LATE = START[WIDE]
REPLICAS = 16
VMEM_KIB = 50176


class Links:
    def __init__(self, send_sems, recv_sems):
        self.send_sems, self.recv_sems = send_sems, recv_sems
        self.index = {}

    def _sem(self, name):
        return self.recv_sems.at[self.index.setdefault(name, len(self.index))]

    def send(self, phase, name, src, dst, target):
        pltpu.make_async_remote_copy(
            src_ref=src, dst_ref=dst, send_sem=self.send_sems.at[phase], recv_sem=self._sem(name),
            device_id=target, device_id_type=MESH,
        ).start()

    def recv(self, name, like):
        pltpu.make_async_copy(like, like, self._sem(name)).wait()

    def sent(self, phase, like):
        pltpu.make_async_copy(like, like, self.send_sems.at[phase]).wait()


AVERAGE_KIB = sum(
    SIZE[k] * (15 if k < WIDE else 10 if k < N - FAST else 8) // 4 for k in range(N)
)
N_MESSAGES = 10 * C + 14 * N - 2 * FAST


def kernel(
    tok_hbm, tgt_hbm, gp_hbm, dr_hbm, m_hbm, v_hbm, om_hbm, new_global, new_momentum,
    tok, tokt, w, tgt, gp, dr, mo, ve, om,
    r_b1, r_b2, r_b3, r_b4, r_d1, r_d2, delta, r_c, r_x, r_z, avg,
    late_sum, late_x, late_f, late_avg,
    load_sem, part_sem, send_sems, recv_sems,
):
    rep = lax.axis_index("replica")
    me = lax.axis_index("fsdp")
    zh, x, c = rep // 8, (rep // 2) % 4, rep % 2
    y, zl = me // 2, me % 2
    yp, ym, y2 = (y + 1) % 4, (y + 3) % 4, (y + 2) % 4
    oz = 1 - zl

    def shard(a, b):
        return a * 2 + b

    to_yp, to_ym = (rep, shard(yp, zl)), (rep, shard(ym, zl))
    to_z = (rep, shard(y, oz))
    to_x = [(zh * 8 + ((x + k) % 4) * 2 + c, me) for k in range(4)]
    to_zh = ((1 - zh) * 8 + x * 2 + c, me)
    to_xc = [(zh * 8 + ((x + k) % 4) * 2 + (1 - c), me) for k in range(4)]
    friends = [to_yp, to_ym, to_z, to_zh] + to_x[1:] + to_xc
    links = Links(send_sems, recv_sems)
    ydirs = ((0, to_yp, ym, yp), (1, to_ym, yp, ym))

    parts = []
    for k in range(C):
        rows = pl.ds(k * R, R)
        a = pltpu.make_async_copy(gp_hbm.at[rows], gp.at[rows], part_sem.at[0, k])
        b = pltpu.make_async_copy(dr_hbm.at[0, rows], dr.at[rows], part_sem.at[1, k])
        a.start()
        b.start()
        parts.append((a, b))
    load_tok = pltpu.make_async_copy(tok_hbm.at[0], tok, load_sem.at[0])
    load_tgt = pltpu.make_async_copy(tgt_hbm.at[0], tgt, load_sem.at[1])
    load_m = pltpu.make_async_copy(m_hbm.at[0], mo, load_sem.at[2])
    load_v = pltpu.make_async_copy(v_hbm.at[0], ve, load_sem.at[3])
    load_om = pltpu.make_async_copy(om_hbm, om, load_sem.at[4])
    for copy in (load_tok, load_tgt, load_m, load_v, load_om):
        copy.start()

    barrier = pltpu.get_barrier_semaphore()
    for friend in friends:
        pl.semaphore_signal(barrier, inc=1, device_id=friend, device_id_type=MESH)

    def weights(k):
        for copy in parts[k]:
            copy.wait()
        rows = pl.ds(k * R, R)
        for h in range(2):
            cols = pl.ds(h * H, H)
            w[me, h, rows] = (gp[rows, cols] + dr[rows, cols]).astype(BF16)

    weights(0)
    pl.semaphore_wait(barrier, len(friends))

    def wpiece(s, k, part=None, h=None):
        rows = pl.ds(k * R, R) if part is None else pl.ds(k * R + (AP[0] if part else 0), AP[part])
        return w.at[s, :, rows] if h is None else w.at[s, h, rows]

    def wsend(name, piece, target):
        links.send(0, name, piece, piece, target)

    for k in range(C):
        if k:
            weights(k)
        for h, target, _, _ in ydirs:
            wsend(("a1", h, k), wpiece(me, k), target)
        wsend(("za", k), wpiece(me, k), to_z)

    load_tok.wait()
    keys = delta.at[:, pl.ds(0, TOK)]

    def dot_keys(s, k):
        cols = pl.ds(pl.multiple_of(s * ROWS + k * R, R), R)
        for h in range(2):
            keys[h] += jnp.dot(tok[:, cols], w[s, h, pl.ds(k * R, R)], preferred_element_type=F32)

    own_cols = pl.ds(pl.multiple_of(me * ROWS, ROWS), ROWS)
    for h in range(2):
        keys[h] = jnp.dot(tok[:, own_cols], w[me, h], preferred_element_type=F32)

    @pl.loop(0, D // 256)
    def _(b):
        at = pl.ds(pl.multiple_of(b * 256, 256), 256)
        tokt[at, :] = tok[:, at].T

    for k in range(C):
        links.recv(("za", k), wpiece(shard(y, oz), k))
        for h, target, _, _ in ydirs:
            wsend(("a2", h, k), wpiece(shard(y, oz), k, 0), target)
        for h, target, src, _ in ydirs:
            links.recv(("a1", h, k), wpiece(shard(src, zl), k))
            wsend(("a3", h, k), wpiece(shard(src, zl), k, None, h), target)
            wsend(("z3", k), wpiece(shard(src, zl), k, 1), to_z)
        dot_keys(shard(y, oz), k)
        dot_keys(shard(ym, zl), k)
        dot_keys(shard(yp, zl), k)
    for k in range(C):
        for h, target, src, _ in ydirs:
            links.recv(("a3", h, k), wpiece(shard(y2, zl), k, None, h))
            wsend(("z5", k), wpiece(shard(y2, zl), k, 1, h), to_z)
        for h, target, src, _ in ydirs:
            links.recv(("a2", h, k), wpiece(shard(src, oz), k, 0))
            wsend(("a4", k), wpiece(shard(src, oz), k, 0, h), target)
        dot_keys(shard(y2, zl), k)
    for k in range(C):
        links.recv(("z3", k), w.at[pl.ds(0, 2), :, pl.ds(0, AP[1])])
        dot_keys(shard(ym, oz), k)
        dot_keys(shard(yp, oz), k)
        links.recv(("z5", k), wpiece(shard(y2, oz), k, 1))
        links.recv(("a4", k), wpiece(shard(y2, oz), k, 0))
        dot_keys(shard(y2, oz), k)

    load_tgt.wait()
    for h in range(2):
        cols = pl.ds(h * H, H)
        tgt[:, cols] = (keys[h] - tgt[:, cols].astype(F32)).astype(BF16)

    links.sent(0, w.at[pl.ds(0, NS - 1)])
    g = w

    def grads(s, k):
        at = pl.ds(pl.multiple_of(s * ROWS + START[k], 16), SIZE[k])
        for h in range(2):
            g[s, h, pl.ds(START[k], SIZE[k])] = jnp.dot(
                tokt[at, :], tgt[:, pl.ds(h * H, H)], preferred_element_type=F32
            ).astype(BF16)

    def grows(k, part):
        return pl.ds(START[k] + (GROUPS[k][0] if part else 0), GROUPS[k][part])

    def gpiece(s, k, part, h=None):
        return g.at[s, :, grows(k, part)] if h is None else g.at[s, h, grows(k, part)]

    def gpair(a, k, h=None):
        two = pl.ds(pl.multiple_of(a * 2, 2), 2)
        return g.at[two, :, grows(k, 0)] if h is None else g.at[two, h, grows(k, 0)]

    def part_rows(k, part):
        return pl.ds(PSTART[part][k], GROUPS[k][part])

    def s1a(k):
        for z in range(2):
            grads(shard(y2, z), k)
        for h, target, _, _ in ydirs:
            links.send(1, ("b1", h, k), gpair(y2, k, h), r_b1.at[h, :, part_rows(k, 0)], target)
        links.send(1, ("da", k), gpiece(shard(y2, oz), k, 1), r_d1.at[3, :, part_rows(k, 1)], to_z)

    def s1b(k):
        @pl.loop(0, 2)
        def _(z):
            for a in (yp, ym, y):
                grads(shard(a, z), k)

        for j, a in ((0, yp), (1, ym), (2, y)):
            links.send(1, ("db", k), gpiece(shard(a, oz), k, 1), r_d1.at[j, :, part_rows(k, 1)], to_z)

    def s2y(h, k):
        p = part_rows(k, 0)
        _, target, _, dst = ydirs[h]
        links.recv(("b1", h, k), r_b1.at[h, :, p])
        own = gpair(dst, k, h)
        own[...] += r_b1[h, :, p]
        links.send(1, ("b2", k), gpair(dst, k), r_b2.at[h, :, :, p], target)

    def s2z(k):
        p = part_rows(k, 1)
        links.recv(("da", k), r_d1.at[3, :, p])
        own = gpiece(shard(y2, zl), k, 1)
        own[...] += r_d1[3, :, p]
        for h, target, _, _ in ydirs:
            links.send(1, ("b3", h, k), gpiece(shard(y2, zl), k, 1, h), r_b3.at[h, p], target)

    have_db = set()

    def s3y(h, k):
        p = part_rows(k, 1)
        _, target, _, dst = ydirs[h]
        if k not in have_db:
            have_db.add(k)
            links.recv(("db", k), r_d1.at[pl.ds(0, 3), :, p])
        links.recv(("b3", h, k), r_b3.at[h, p])
        one = gpiece(shard(dst, zl), k, 1, h)
        one[...] += r_d1[h, h, p] + r_b3[h, p]
        two = gpiece(shard(dst, zl), k, 1, 1 - h)
        two[...] += r_d1[h, 1 - h, p]
        links.send(1, ("b4", k), gpiece(shard(dst, zl), k, 1), r_b4.at[h, :, p], target)

    def s3z(k):
        p = part_rows(k, 0)
        links.recv(("b2", k), r_b2.at[:, :, :, p])
        own = gpiece(shard(y, oz), k, 0)
        own[...] += r_b2[0, oz, :, p] + r_b2[1, oz, :, p]
        links.send(1, ("d2", k), own, r_d2.at[:, p], to_z)

    def update(rows, cols, grad_sum):
        grad = grad_sum * (1.0 / (TOK * NS))
        glob = gp[rows, cols]
        local = glob + dr[rows, cols]
        moment = 0.9 * mo[rows, cols] + 0.1 * grad
        second = 0.95 * ve[rows, cols] + 0.05 * grad * grad
        step = moment / corr_one / (jnp.sqrt(second / corr_two) + 1e-08) + 0.1 * local
        return glob - (local - 0.003 * step)

    def updates(k, part, total):
        sub = next(b for b in (48, 32, 16) if GROUPS[k][part] % b == 0)

        @pl.loop(0, GROUPS[k][part] // sub)
        def _(i):
            off = pl.multiple_of(i * sub, 16)
            rows = pl.ds(START[k] + (GROUPS[k][0] if part else 0) + off, sub)
            p = pl.ds(PSTART[part][k] + off, sub)
            for h in range(2):
                delta[h, rows] = update(rows, pl.ds(h * H, H), total(h, rows, p))

    def s4(k):
        if k == 0:
            load_m.wait()
            load_v.wait()
        links.recv(("d2", k), r_d2.at[:, part_rows(k, 0)])
        updates(
            k, 0,
            lambda h, rows, p: (g[me, h, rows].astype(F32) + r_d2[h, p].astype(F32))
            + (r_b2[0, zl, h, p].astype(F32) + r_b2[1, zl, h, p].astype(F32)),
        )
        links.recv(("b4", k), r_b4.at[:, :, part_rows(k, 1)])
        updates(
            k, 1,
            lambda h, rows, p: (g[me, h, rows].astype(F32) + r_d1[2, h, p].astype(F32))
            + (r_b4[0, h, p].astype(F32) + r_b4[1, h, p].astype(F32)),
        )
        if k < N - FAST:
            rows = pl.ds(START[k], SIZE[k])
            links.send(2, ("c", k), delta.at[1 - c, rows], r_c.at[rows], to_xc[0])
        else:
            rows = pl.ds(START[k], SIZE[k])
            late_sum[:, pl.ds(START[k] - LATE, SIZE[k])] = delta[:, rows].astype(BF16)
            for j, other, target in others():
                half = 1 - c if other else c
                links.send(
                    2, ("x", k), late_sum.at[half, late_rows(k, (x + j) % 4)], f_slot(j, other, k), target
                )

    def others():
        found = [(j, 0, to_x[j]) for j in (2, 1, 3)] + [(j, 1, to_xc[j]) for j in (2, 1, 3, 0)]
        return sorted(found, key=lambda f: (2, 1, 3, 0).index(f[0]))

    def x_rows(k, a):
        q = SIZE[k] // 4
        return pl.ds(pl.multiple_of(START[k] + a * q, 8), q)

    def late_rows(k, a):
        q = SIZE[k] // 4
        return pl.ds(pl.multiple_of(START[k] - LATE + a * q, 16), q)

    def q_rows(k):
        return pl.ds(START[k] // 4, SIZE[k] // 4)

    def x_slots(k):
        if k < WIDE:
            return r_x.at[:, q_rows(k)]
        return late_x.at[:, pl.ds((START[k] - LATE) // 4, SIZE[k] // 4)]

    def f_slot(j, other, k):
        q = SIZE[k] // 4
        return late_f.at[j * 2 + other, pl.ds((START[k] - START[N - FAST]) // 4, q)]

    def f_slots(k):
        q = SIZE[k] // 4
        return late_f.at[pl.ds(1, 7), pl.ds((START[k] - START[N - FAST]) // 4, q)]

    def s5(k):
        rows = pl.ds(START[k], SIZE[k])
        links.recv(("c", k), r_c.at[rows])
        delta[c, rows] += r_c[rows]
        if k >= WIDE:
            late_sum[c, pl.ds(START[k] - LATE, SIZE[k])] = delta[c, rows].astype(BF16)
        for j in (2, 1, 3):
            at = (x + j) % 4
            piece = delta.at[c, x_rows(k, at)] if k < WIDE else late_sum.at[c, late_rows(k, at)]
            links.send(2, ("x", k), piece, x_slots(k).at[j - 1], to_x[j])

    def s6(k):
        at = x_rows(k, x)
        if k < N - FAST:
            got = x_slots(k)
            links.recv(("x", k), got)
            delta[c, at] += got[0].astype(F32) + got[1].astype(F32) + got[2].astype(F32)
        else:
            links.recv(("x", k), f_slots(k))
            total = delta[c, at]
            for j, other, _ in others():
                total += f_slot(j, other, k)[...].astype(F32)
            delta[c, at] = total
        links.send(2, ("zh", k), delta.at[c, at], r_z.at[q_rows(k)], to_zh)

    def s7(k):
        links.recv(("zh", k), r_z.at[q_rows(k)])
        at = x_rows(k, x)
        average = (delta[c, at] + r_z[q_rows(k)]) * (1.0 / REPLICAS)
        if k < WIDE:
            piece = avg.at[c, at]
            piece[...] = average
        else:
            piece = late_avg.at[c, late_rows(k, x)]
            piece[...] = average.astype(BF16)
        if k < N - FAST:
            for j in (2, 1, 3):
                links.send(2, ("xg", k), piece, piece, to_x[j])
        else:
            for j, other, target in others():
                links.send(2, ("xg", k), piece, piece, target)

    def averages(half, k):
        if k < WIDE:
            return avg.at[half, pl.ds(START[k], SIZE[k])]
        return late_avg.at[half, pl.ds(START[k] - LATE, SIZE[k])]

    def outer(k, half):
        sub = 32

        @pl.loop(0, SIZE[k] // sub)
        def _(i):
            off = pl.multiple_of(i * sub, sub)
            rows = pl.ds(START[k] + off, sub)
            cols = pl.ds(pl.multiple_of(half * H, H), H)
            average = averages(half, k)[pl.ds(off, sub)].astype(F32)
            momentum_next = 0.9 * om[rows, cols] + average
            new_momentum[rows, cols] = momentum_next
            new_global[rows, cols] = gp[rows, cols] - 0.7 * (0.9 * momentum_next + average)

    def s8(k):
        links.recv(("xg", k), x_slots(k))
        links.send(2, ("cg", k), averages(c, k), averages(c, k), to_xc[0])
        if k == 0:
            load_om.wait()
        outer(k, c)

    def s9(k):
        if k < N - FAST:
            links.recv(("cg", k), averages(1 - c, k))
            outer(k, 1 - c)
        else:
            links.recv(("xg", k), f_slots(k))
            outer(k, 0)
            outer(k, 1)

    s2y0, s2y1 = functools.partial(s2y, 0), functools.partial(s2y, 1)
    s3y0, s3y1 = functools.partial(s3y, 0), functools.partial(s3y, 1)
    order = (
        (s1a, 4), (s1a, 0), (s1b, 0), (s1a, 2), (s2z, 0), (s1a, 1), (s1a, 3), (s2y1, 0), (s2y0, 0), (s1b, 1),
        (s2y0, 1), (s1b, 2), (s2y1, 1), (s3z, 0), (s2z, 1), (s3y1, 0), (s2y1, 2), (s3y0, 0), (s3z, 1),
        (s2y0, 2), (s3y0, 1), (s1b, 4), (s1b, 3), (s2y0, 3), (s3y1, 1), (s4, 0), (s2z, 2), (s2y1, 3), (s5, 0),
        (s3z, 2), (s4, 1), (s2z, 3), (s1a, 5), (s3y1, 2), (s2y0, 4), (s6, 0), (s3y0, 2), (s2y1, 4), (s3z, 3),
        (s5, 1), (s2z, 4), (s3y1, 3), (s3y0, 3), (s2z, 5), (s1b, 5), (s2y0, 5), (s7, 0), (s2y1, 5), (s4, 2),
        (s3y0, 4), (s3z, 4), (s3y1, 4), (s6, 1), (s4, 3), (s5, 2), (s3y1, 5), (s3y0, 5), (s3z, 5), (s4, 4),
        (s5, 3), (s5, 4), (s6, 2), (s4, 5), (s8, 0), (s7, 1), (s6, 3), (s6, 4), (s6, 5), (s7, 2), (s7, 3),
        (s8, 1), (s7, 4), (s7, 5), (s9, 0), (s8, 2), (s9, 1), (s8, 3), (s8, 4), (s9, 2), (s9, 5), (s9, 3),
        (s9, 4),
    )
    for stage, k in order:
        stage(k)
    links.sent(1, tokt.at[pl.ds(0, (NS - 1) * ROWS)])
    links.sent(2, tokt.at[pl.ds(0, AVERAGE_KIB)])


def step(*arrays):
    in_hbm = pl.BlockSpec(memory_space=pltpu.HBM)
    in_vmem = pl.BlockSpec(memory_space=pltpu.VMEM)
    p1, p2 = PROWS
    return pl.pallas_call(
        kernel,
        out_shape=(jax.ShapeDtypeStruct((ROWS, KV), F32),) * 2,
        in_specs=[in_hbm] * 7,
        out_specs=(in_vmem, in_vmem),
        scratch_shapes=[
            pltpu.VMEM((TOK, D), BF16),
            pltpu.VMEM((D, TOK), BF16),
            pltpu.VMEM((NS, 2, ROWS, H), BF16),
            pltpu.VMEM((TOK, KV), BF16),
            pltpu.VMEM((ROWS, KV), F32),
            pltpu.VMEM((ROWS, KV), F32),
            pltpu.VMEM((ROWS, KV), F32),
            pltpu.VMEM((ROWS, KV), F32),
            pltpu.VMEM((ROWS, KV), F32),
            pltpu.VMEM((2, 2, p1, H), BF16),
            pltpu.VMEM((2, 2, 2, p1, H), BF16),
            pltpu.VMEM((2, p2, H), BF16),
            pltpu.VMEM((2, 2, p2, H), BF16),
            pltpu.VMEM((4, 2, p2, H), BF16),
            pltpu.VMEM((2, p1, H), BF16),
            pltpu.VMEM((2, ROWS, H), F32),
            pltpu.VMEM((ROWS, H), F32),
            pltpu.VMEM((3, LATE // 4, H), F32),
            pltpu.VMEM((ROWS // 4, H), F32),
            pltpu.VMEM((2, LATE, H), F32),
            pltpu.VMEM((2, ROWS - LATE, H), BF16),
            pltpu.VMEM((3, (ROWS - LATE) // 4, H), BF16),
            pltpu.VMEM((8, sum(SIZE[N - FAST :]) // 4, H), BF16),
            pltpu.VMEM((2, ROWS - LATE, H), BF16),
            pltpu.SemaphoreType.DMA((5,)),
            pltpu.SemaphoreType.DMA((2, C)),
            pltpu.SemaphoreType.DMA((3,)),
            pltpu.SemaphoreType.DMA((N_MESSAGES,)),
        ],
        compiler_params=pltpu.CompilerParams(
            collective_id=0, has_side_effects=True, vmem_limit_bytes=VMEM_KIB * 2**10
        ),
        cost_estimate=pl.CostEstimate(
            flops=4 * TOK * D * KV, bytes_accessed=24 * 2**20, transcendentals=ROWS * KV
        ),
        name="inner_and_outer_step",
    )(*(pltpu.with_memory_space_constraint(a, pltpu.HBM) for a in arrays))


def write_kernel(a_ref, b_ref, a_hbm, b_hbm, sems):
    copies = []
    for i, (src, dst) in enumerate(((a_ref, a_hbm), (b_ref, b_hbm))):
        for q in range(2):
            rows = pl.ds(q * ROWS // 2, ROWS // 2)
            copies.append(pltpu.make_async_copy(src.at[rows], dst.at[rows], sems.at[i, q]))
    for copy in copies:
        copy.start()
    for copy in copies:
        copy.wait()


def whole(*arrays):
    return pl.pallas_call(
        write_kernel,
        out_shape=(jax.ShapeDtypeStruct((ROWS, KV), F32),) * 2,
        in_specs=[pl.BlockSpec(memory_space=pl.ANY)] * 2,
        out_specs=(pl.BlockSpec(memory_space=pltpu.HBM),) * 2,
        scratch_shapes=[pltpu.SemaphoreType.DMA((2, 2))],
        compiler_params=pltpu.CompilerParams(vmem_limit_bytes=2**20),
        name="write_results",
    )(*step(*arrays))


def solution(mesh):
    in_specs = (
        P("replica", "fsdp", None),
        P("replica", "fsdp", None),
        P("fsdp", None),
        P("replica", "fsdp", None),
        P("replica", "fsdp", None),
        P("replica", "fsdp", None),
        P("fsdp", None),
    )
    out_specs = (P("fsdp", None), P("fsdp", None))
    return jax.shard_map(whole, mesh=mesh, in_specs=in_specs, out_specs=out_specs, check_vma=False)
```

```python
import functools
import jax
import jax.numpy as jnp
from jax import lax
from jax.experimental import pallas as pl
from jax.experimental.pallas import tpu as pltpu
from jax.sharding import PartitionSpec as P

MESH = pl.DeviceIdType.MESH
F32 = jnp.float32
BF16 = jnp.bfloat16

corr_one = 1.0 - 0.9**20
corr_two = 1.0 - 0.95**20

TOK = 512
D = 8192
KV = 512
NS = 8
ROWS = D // NS
H = KV // 2
C = 4
R = ROWS // C
AP = (144, 112)
GROUPS = ((160, 96), (144, 112), (112, 80), (112, 80), (32, 32), (32, 32))
N = len(GROUPS)
FAST = 1
SIZE = [sum(p) for p in GROUPS]
START = [sum(SIZE[:k]) for k in range(N)]
PSTART = [[sum(p[i] for p in GROUPS[:k]) for k in range(N)] for i in range(2)]
PROWS = [sum(p[i] for p in GROUPS) for i in range(2)]
REPLICAS = 16
VMEM_KIB = 50176


class Links:
    def __init__(self, send_sems, recv_sems):
        self.send_sems, self.recv_sems = send_sems, recv_sems
        self.index = {}

    def _sem(self, name):
        return self.recv_sems.at[self.index.setdefault(name, len(self.index))]

    def send(self, phase, name, src, dst, target):
        pltpu.make_async_remote_copy(
            src_ref=src, dst_ref=dst, send_sem=self.send_sems.at[phase], recv_sem=self._sem(name),
            device_id=target, device_id_type=MESH,
        ).start()

    def recv(self, name, like):
        pltpu.make_async_copy(like, like, self._sem(name)).wait()

    def sent(self, phase, like):
        pltpu.make_async_copy(like, like, self.send_sems.at[phase]).wait()


N_MESSAGES = 10 * C + 14 * N - 2 * FAST


def kernel(
    tok_hbm, tgt_hbm, gp_hbm, dr_hbm, m_hbm, v_hbm, om_hbm, new_global, new_momentum,
    tok, tokt, w, tgt, gp, dr, mo, ve, om,
    r_b1, r_b2, r_b3, r_b4, r_d1, r_d2, delta, r_c, r_x, r_z, r_f, avg,
    load_sem, part_sem, send_sems, recv_sems,
):
    rep = lax.axis_index("replica")
    me = lax.axis_index("fsdp")
    zh, x, c = rep // 8, (rep // 2) % 4, rep % 2
    y, zl = me // 2, me % 2
    yp, ym, y2 = (y + 1) % 4, (y + 3) % 4, (y + 2) % 4
    oz = 1 - zl

    def shard(a, b):
        return a * 2 + b

    to_yp, to_ym = (rep, shard(yp, zl)), (rep, shard(ym, zl))
    to_z = (rep, shard(y, oz))
    to_x = [(zh * 8 + ((x + k) % 4) * 2 + c, me) for k in range(4)]
    to_zh = ((1 - zh) * 8 + x * 2 + c, me)
    to_xc = [(zh * 8 + ((x + k) % 4) * 2 + (1 - c), me) for k in range(4)]
    friends = [to_yp, to_ym, to_z, to_zh] + to_x[1:] + to_xc
    links = Links(send_sems, recv_sems)
    ydirs = ((0, to_yp, ym, yp), (1, to_ym, yp, ym))

    parts = []
    for k in range(C):
        rows = pl.ds(k * R, R)
        a = pltpu.make_async_copy(gp_hbm.at[rows], gp.at[rows], part_sem.at[0, k])
        b = pltpu.make_async_copy(dr_hbm.at[0, rows], dr.at[rows], part_sem.at[1, k])
        a.start()
        b.start()
        parts.append((a, b))
    load_tok = pltpu.make_async_copy(tok_hbm.at[0], tok, load_sem.at[0])
    load_tgt = pltpu.make_async_copy(tgt_hbm.at[0], tgt, load_sem.at[1])
    load_m = pltpu.make_async_copy(m_hbm.at[0], mo, load_sem.at[2])
    load_v = pltpu.make_async_copy(v_hbm.at[0], ve, load_sem.at[3])
    load_om = pltpu.make_async_copy(om_hbm, om, load_sem.at[4])
    for copy in (load_tok, load_tgt, load_m, load_v, load_om):
        copy.start()

    barrier = pltpu.get_barrier_semaphore()
    for friend in friends:
        pl.semaphore_signal(barrier, inc=1, device_id=friend, device_id_type=MESH)

    def weights(k):
        for copy in parts[k]:
            copy.wait()
        rows = pl.ds(k * R, R)
        for h in range(2):
            cols = pl.ds(h * H, H)
            w[me, h, rows] = (gp[rows, cols] + dr[rows, cols]).astype(BF16)

    weights(0)
    pl.semaphore_wait(barrier, len(friends))

    def wpiece(s, k, part=None, h=None):
        rows = pl.ds(k * R, R) if part is None else pl.ds(k * R + (AP[0] if part else 0), AP[part])
        return w.at[s, :, rows] if h is None else w.at[s, h, rows]

    def wsend(name, piece, target):
        links.send(0, name, piece, piece, target)

    for k in range(C):
        if k:
            weights(k)
        for h, target, _, _ in ydirs:
            wsend(("a1", h, k), wpiece(me, k), target)
        wsend(("za", k), wpiece(me, k), to_z)

    load_tok.wait()
    keys = delta.at[:, pl.ds(0, TOK)]

    def dot_keys(s, k):
        cols = pl.ds(pl.multiple_of(s * ROWS + k * R, R), R)
        for h in range(2):
            keys[h] += jnp.dot(tok[:, cols], w[s, h, pl.ds(k * R, R)], preferred_element_type=F32)

    own_cols = pl.ds(pl.multiple_of(me * ROWS, ROWS), ROWS)
    for h in range(2):
        keys[h] = jnp.dot(tok[:, own_cols], w[me, h], preferred_element_type=F32)

    @pl.loop(0, D // 256)
    def _(b):
        at = pl.ds(pl.multiple_of(b * 256, 256), 256)
        tokt[at, :] = tok[:, at].T

    for k in range(C):
        links.recv(("za", k), wpiece(shard(y, oz), k))
        for h, target, _, _ in ydirs:
            wsend(("a2", h, k), wpiece(shard(y, oz), k, 0), target)
        for h, target, src, _ in ydirs:
            links.recv(("a1", h, k), wpiece(shard(src, zl), k))
            wsend(("a3", h, k), wpiece(shard(src, zl), k, None, h), target)
            wsend(("z3", k), wpiece(shard(src, zl), k, 1), to_z)
        dot_keys(shard(y, oz), k)
        dot_keys(shard(ym, zl), k)
        dot_keys(shard(yp, zl), k)
    for k in range(C):
        for h, target, src, _ in ydirs:
            links.recv(("a3", h, k), wpiece(shard(y2, zl), k, None, h))
            wsend(("z5", k), wpiece(shard(y2, zl), k, 1, h), to_z)
        for h, target, src, _ in ydirs:
            links.recv(("a2", h, k), wpiece(shard(src, oz), k, 0))
            wsend(("a4", k), wpiece(shard(src, oz), k, 0, h), target)
        dot_keys(shard(y2, zl), k)
    for k in range(C):
        links.recv(("z3", k), w.at[pl.ds(0, 2), :, pl.ds(0, AP[1])])
        dot_keys(shard(ym, oz), k)
        dot_keys(shard(yp, oz), k)
        links.recv(("z5", k), wpiece(shard(y2, oz), k, 1))
        links.recv(("a4", k), wpiece(shard(y2, oz), k, 0))
        dot_keys(shard(y2, oz), k)

    load_tgt.wait()
    for h in range(2):
        cols = pl.ds(h * H, H)
        tgt[:, cols] = (keys[h] - tgt[:, cols].astype(F32)).astype(BF16)

    links.sent(0, w.at[pl.ds(0, NS - 1)])
    g = w

    def grads(s, k):
        at = pl.ds(pl.multiple_of(s * ROWS + START[k], 16), SIZE[k])
        for h in range(2):
            g[s, h, pl.ds(START[k], SIZE[k])] = jnp.dot(
                tokt[at, :], tgt[:, pl.ds(h * H, H)], preferred_element_type=F32
            ).astype(BF16)

    def grows(k, part):
        return pl.ds(START[k] + (GROUPS[k][0] if part else 0), GROUPS[k][part])

    def gpiece(s, k, part, h=None):
        return g.at[s, :, grows(k, part)] if h is None else g.at[s, h, grows(k, part)]

    def gpair(a, k, h=None):
        two = pl.ds(pl.multiple_of(a * 2, 2), 2)
        return g.at[two, :, grows(k, 0)] if h is None else g.at[two, h, grows(k, 0)]

    def part_rows(k, part):
        return pl.ds(PSTART[part][k], GROUPS[k][part])

    def s1a(k):
        for z in range(2):
            grads(shard(y2, z), k)
        for h, target, _, _ in ydirs:
            links.send(1, ("b1", h, k), gpair(y2, k, h), r_b1.at[h, :, part_rows(k, 0)], target)
        links.send(1, ("da", k), gpiece(shard(y2, oz), k, 1), r_d1.at[3, :, part_rows(k, 1)], to_z)

    def s1b(k):
        @pl.loop(0, 2)
        def _(z):
            for a in (yp, ym, y):
                grads(shard(a, z), k)

        for j, a in ((0, yp), (1, ym), (2, y)):
            links.send(1, ("db", k), gpiece(shard(a, oz), k, 1), r_d1.at[j, :, part_rows(k, 1)], to_z)

    def s2y(h, k):
        p = part_rows(k, 0)
        _, target, _, dst = ydirs[h]
        links.recv(("b1", h, k), r_b1.at[h, :, p])
        own = gpair(dst, k, h)
        own[...] += r_b1[h, :, p]
        links.send(1, ("b2", k), gpair(dst, k), r_b2.at[h, :, :, p], target)

    def s2z(k):
        p = part_rows(k, 1)
        links.recv(("da", k), r_d1.at[3, :, p])
        own = gpiece(shard(y2, zl), k, 1)
        own[...] += r_d1[3, :, p]
        for h, target, _, _ in ydirs:
            links.send(1, ("b3", h, k), gpiece(shard(y2, zl), k, 1, h), r_b3.at[h, p], target)

    have_db = set()

    def s3y(h, k):
        p = part_rows(k, 1)
        _, target, _, dst = ydirs[h]
        if k not in have_db:
            have_db.add(k)
            links.recv(("db", k), r_d1.at[pl.ds(0, 3), :, p])
        links.recv(("b3", h, k), r_b3.at[h, p])
        one = gpiece(shard(dst, zl), k, 1, h)
        one[...] += r_d1[h, h, p] + r_b3[h, p]
        two = gpiece(shard(dst, zl), k, 1, 1 - h)
        two[...] += r_d1[h, 1 - h, p]
        links.send(1, ("b4", k), gpiece(shard(dst, zl), k, 1), r_b4.at[h, :, p], target)

    def s3z(k):
        p = part_rows(k, 0)
        links.recv(("b2", k), r_b2.at[:, :, :, p])
        own = gpiece(shard(y, oz), k, 0)
        own[...] += r_b2[0, oz, :, p] + r_b2[1, oz, :, p]
        links.send(1, ("d2", k), own, r_d2.at[:, p], to_z)

    def update(rows, cols, grad_sum):
        grad = grad_sum * (1.0 / (TOK * NS))
        glob = gp[rows, cols]
        local = glob + dr[rows, cols]
        moment = 0.9 * mo[rows, cols] + 0.1 * grad
        second = 0.95 * ve[rows, cols] + 0.05 * grad * grad
        step = moment / corr_one / (jnp.sqrt(second / corr_two) + 1e-08) + 0.1 * local
        return glob - (local - 0.003 * step)

    def updates(k, part, total):
        sub = next(b for b in (48, 32, 16) if GROUPS[k][part] % b == 0)

        @pl.loop(0, GROUPS[k][part] // sub)
        def _(i):
            off = pl.multiple_of(i * sub, 16)
            rows = pl.ds(START[k] + (GROUPS[k][0] if part else 0) + off, sub)
            p = pl.ds(PSTART[part][k] + off, sub)
            for h in range(2):
                delta[h, rows] = update(rows, pl.ds(h * H, H), total(h, rows, p))

    def s4(k):
        links.recv(("d2", k), r_d2.at[:, part_rows(k, 0)])
        updates(
            k, 0,
            lambda h, rows, p: (g[me, h, rows].astype(F32) + r_d2[h, p].astype(F32))
            + (r_b2[0, zl, h, p].astype(F32) + r_b2[1, zl, h, p].astype(F32)),
        )
        links.recv(("b4", k), r_b4.at[:, :, part_rows(k, 1)])
        updates(
            k, 1,
            lambda h, rows, p: (g[me, h, rows].astype(F32) + r_d1[2, h, p].astype(F32))
            + (r_b4[0, h, p].astype(F32) + r_b4[1, h, p].astype(F32)),
        )
        if k < N - FAST:
            rows = pl.ds(START[k], SIZE[k])
            links.send(2, ("c", k), delta.at[1 - c, rows], r_c.at[rows], to_xc[0])
        else:
            for j, other, target in others():
                half = 1 - c if other else c
                links.send(
                    2, ("x", k), delta.at[half, x_rows(k, (x + j) % 4)], f_slot(j, other, k), target
                )

    def others():
        found = [(j, 0, to_x[j]) for j in (2, 1, 3)] + [(j, 1, to_xc[j]) for j in (2, 1, 3, 0)]
        return sorted(found, key=lambda f: (2, 1, 3, 0).index(f[0]))

    def x_rows(k, a):
        q = SIZE[k] // 4
        return pl.ds(pl.multiple_of(START[k] + a * q, 8), q)

    def q_rows(k):
        return pl.ds(START[k] // 4, SIZE[k] // 4)

    def f_slot(j, other, k):
        q = SIZE[k] // 4
        return r_f.at[j * 2 + other, pl.ds((START[k] - START[N - FAST]) // 4, q)]

    def f_slots(k):
        q = SIZE[k] // 4
        return r_f.at[pl.ds(1, 7), pl.ds((START[k] - START[N - FAST]) // 4, q)]

    def s5(k):
        rows = pl.ds(START[k], SIZE[k])
        links.recv(("c", k), r_c.at[rows])
        delta[c, rows] += r_c[rows]
        for j in (2, 1, 3):
            links.send(
                2, ("x", k), delta.at[c, x_rows(k, (x + j) % 4)], r_x.at[j - 1, q_rows(k)], to_x[j]
            )

    def s6(k):
        at = x_rows(k, x)
        if k < N - FAST:
            p = q_rows(k)
            links.recv(("x", k), r_x.at[:, p])
            delta[c, at] += r_x[0, p] + r_x[1, p] + r_x[2, p]
        else:
            links.recv(("x", k), f_slots(k))
            total = delta[c, at]
            for j, other, _ in others():
                total += f_slot(j, other, k)[...]
            delta[c, at] = total
        links.send(2, ("zh", k), delta.at[c, at], r_z.at[q_rows(k)], to_zh)

    def s7(k):
        links.recv(("zh", k), r_z.at[q_rows(k)])
        at = x_rows(k, x)
        avg[c, at] = (delta[c, at] + r_z[q_rows(k)]) * (1.0 / REPLICAS)
        if k < N - FAST:
            for j in (2, 1, 3):
                links.send(2, ("xg", k), avg.at[c, at], avg.at[c, at], to_x[j])
        else:
            for j, other, target in others():
                links.send(2, ("xg", k), avg.at[c, at], avg.at[c, at], target)

    def outer(k, half):
        sub = 32

        @pl.loop(0, SIZE[k] // sub)
        def _(i):
            rows = pl.ds(START[k] + pl.multiple_of(i * sub, sub), sub)
            cols = pl.ds(pl.multiple_of(half * H, H), H)
            average = avg[half, rows]
            momentum_next = 0.9 * om[rows, cols] + average
            new_momentum[rows, cols] = momentum_next
            new_global[rows, cols] = gp[rows, cols] - 0.7 * (0.9 * momentum_next + average)

    def s8(k):
        links.recv(("xg", k), r_x.at[:, q_rows(k)])
        rows = pl.ds(START[k], SIZE[k])
        links.send(2, ("cg", k), avg.at[c, rows], avg.at[c, rows], to_xc[0])
        outer(k, c)

    def s9(k):
        if k < N - FAST:
            rows = pl.ds(START[k], SIZE[k])
            links.recv(("cg", k), avg.at[1 - c, rows])
            outer(k, 1 - c)
        else:
            links.recv(("xg", k), f_slots(k))
            outer(k, 0)
            outer(k, 1)

    s2y0, s2y1 = functools.partial(s2y, 0), functools.partial(s2y, 1)
    s3y0, s3y1 = functools.partial(s3y, 0), functools.partial(s3y, 1)
    order = (
        (s1a, 4), (s1a, 2), (s1a, 1), (s1b, 1), (s1a, 3), (s1b, 3), (s1a, 0), (s2z, 1), (s2y1, 1), (s1b, 0),
        (s2y0, 1), (s2y0, 0), (s2y1, 0), (s3z, 1), (s2z, 0), (s2z, 3), (s3y0, 1), (s3y1, 1), (s3z, 0),
        (s2y0, 3), (s2y1, 3), (s3y1, 0), (s3y0, 0), (s1b, 2), (s2z, 2), (s2y0, 2), (s2y1, 2), (s4, 1), (s5, 1),
        (s3y0, 3), (s3y1, 3), (s1b, 4), (s3z, 3), (s4, 0), (s2y1, 4), (s1a, 5), (s6, 1), (s2z, 4), (s5, 0),
        (s2y0, 4), (s3y0, 2), (s3z, 2), (s1b, 5), (s3y1, 2), (s4, 3), (s2z, 5), (s2y0, 5), (s3y0, 4), (s7, 1),
        (s2y1, 5), (s3y1, 4), (s3z, 4), (s6, 0), (s5, 3), (s4, 2), (s3y1, 5), (s3y0, 5), (s3z, 5), (s5, 2),
        (s4, 4), (s5, 4), (s6, 3), (s4, 5), (s7, 0), (s8, 1), (s6, 2), (s7, 3), (s6, 4), (s6, 5), (s7, 2),
        (s8, 0), (s7, 4), (s7, 5), (s8, 3), (s9, 1), (s8, 2), (s9, 0), (s8, 4), (s9, 3), (s9, 5), (s9, 4),
        (s9, 2),
    )
    for copy in (load_m, load_v, load_om):
        copy.wait()
    for stage, k in order:
        stage(k)
    links.sent(1, tokt.at[pl.ds(0, (NS - 1) * ROWS)])
    links.sent(2, tokt.at[pl.ds(0, 15 * ROWS // 4)])


def step(*arrays):
    in_hbm = pl.BlockSpec(memory_space=pltpu.HBM)
    in_vmem = pl.BlockSpec(memory_space=pltpu.VMEM)
    p1, p2 = PROWS
    return pl.pallas_call(
        kernel,
        out_shape=(jax.ShapeDtypeStruct((ROWS, KV), F32),) * 2,
        in_specs=[in_hbm] * 7,
        out_specs=(in_vmem, in_vmem),
        scratch_shapes=[
            pltpu.VMEM((TOK, D), BF16),
            pltpu.VMEM((D, TOK), BF16),
            pltpu.VMEM((NS, 2, ROWS, H), BF16),
            pltpu.VMEM((TOK, KV), BF16),
            pltpu.VMEM((ROWS, KV), F32),
            pltpu.VMEM((ROWS, KV), F32),
            pltpu.VMEM((ROWS, KV), F32),
            pltpu.VMEM((ROWS, KV), F32),
            pltpu.VMEM((ROWS, KV), F32),
            pltpu.VMEM((2, 2, p1, H), BF16),
            pltpu.VMEM((2, 2, 2, p1, H), BF16),
            pltpu.VMEM((2, p2, H), BF16),
            pltpu.VMEM((2, 2, p2, H), BF16),
            pltpu.VMEM((4, 2, p2, H), BF16),
            pltpu.VMEM((2, p1, H), BF16),
            pltpu.VMEM((2, ROWS, H), F32),
            pltpu.VMEM((ROWS, H), F32),
            pltpu.VMEM((3, ROWS // 4, H), F32),
            pltpu.VMEM((ROWS // 4, H), F32),
            pltpu.VMEM((8, sum(SIZE[N - FAST :]) // 4, H), F32),
            pltpu.VMEM((2, ROWS, H), F32),
            pltpu.SemaphoreType.DMA((5,)),
            pltpu.SemaphoreType.DMA((2, C)),
            pltpu.SemaphoreType.DMA((3,)),
            pltpu.SemaphoreType.DMA((N_MESSAGES,)),
        ],
        compiler_params=pltpu.CompilerParams(
            collective_id=0, has_side_effects=True, vmem_limit_bytes=VMEM_KIB * 2**10
        ),
        cost_estimate=pl.CostEstimate(
            flops=4 * TOK * D * KV, bytes_accessed=24 * 2**20, transcendentals=ROWS * KV
        ),
        name="inner_and_outer_step",
    )(*(pltpu.with_memory_space_constraint(a, pltpu.HBM) for a in arrays))


def write_kernel(a_ref, b_ref, a_hbm, b_hbm, sems):
    copies = []
    for i, (src, dst) in enumerate(((a_ref, a_hbm), (b_ref, b_hbm))):
        for q in range(2):
            rows = pl.ds(q * ROWS // 2, ROWS // 2)
            copies.append(pltpu.make_async_copy(src.at[rows], dst.at[rows], sems.at[i, q]))
    for copy in copies:
        copy.start()
    for copy in copies:
        copy.wait()


def whole(*arrays):
    return pl.pallas_call(
        write_kernel,
        out_shape=(jax.ShapeDtypeStruct((ROWS, KV), F32),) * 2,
        in_specs=[pl.BlockSpec(memory_space=pl.ANY)] * 2,
        out_specs=(pl.BlockSpec(memory_space=pltpu.HBM),) * 2,
        scratch_shapes=[pltpu.SemaphoreType.DMA((2, 2))],
        compiler_params=pltpu.CompilerParams(vmem_limit_bytes=2**20),
        name="write_results",
    )(*step(*arrays))


def solution(mesh):
    in_specs = (
        P("replica", "fsdp", None),
        P("replica", "fsdp", None),
        P("fsdp", None),
        P("replica", "fsdp", None),
        P("replica", "fsdp", None),
        P("replica", "fsdp", None),
        P("fsdp", None),
    )
    out_specs = (P("fsdp", None), P("fsdp", None))
    return jax.shard_map(whole, mesh=mesh, in_specs=in_specs, out_specs=out_specs, check_vma=False)
```

```python
import functools
import jax
import jax.numpy as jnp
from jax import lax
from jax.experimental import pallas as pl
from jax.experimental.pallas import tpu as pltpu
from jax.sharding import PartitionSpec as P

MESH = pl.DeviceIdType.MESH
F32 = jnp.float32
BF16 = jnp.bfloat16

corr_one = 1.0 - 0.9**20
corr_two = 1.0 - 0.95**20

TOK = 512
D = 8192
KV = 512
NS = 8
ROWS = D // NS
H = KV // 2
C = 4
R = ROWS // C
AP = (144, 112)
GROUPS = ((160, 96), (144, 112), (112, 80), (112, 80), (32, 32), (32, 32))
N = len(GROUPS)
FAST = 1
SIZE = [sum(p) for p in GROUPS]
START = [sum(SIZE[:k]) for k in range(N)]
PSTART = [[sum(p[i] for p in GROUPS[:k]) for k in range(N)] for i in range(2)]
PROWS = [sum(p[i] for p in GROUPS) for i in range(2)]
WIDE = 3
LATE = START[WIDE]
REPLICAS = 16
VMEM_KIB = 50176


class Links:
    def __init__(self, send_sems, recv_sems):
        self.send_sems, self.recv_sems = send_sems, recv_sems
        self.index = {}

    def _sem(self, name):
        return self.recv_sems.at[self.index.setdefault(name, len(self.index))]

    def send(self, phase, name, src, dst, target):
        pltpu.make_async_remote_copy(
            src_ref=src, dst_ref=dst, send_sem=self.send_sems.at[phase], recv_sem=self._sem(name),
            device_id=target, device_id_type=MESH,
        ).start()

    def recv(self, name, like):
        pltpu.make_async_copy(like, like, self._sem(name)).wait()

    def sent(self, phase, like):
        pltpu.make_async_copy(like, like, self.send_sems.at[phase]).wait()


AVERAGE_KIB = sum(
    SIZE[k] * (15 if k < WIDE else 10 if k < N - FAST else 8) // 4 for k in range(N)
)
N_MESSAGES = 10 * C + 14 * N - 2 * FAST


def kernel(
    tok_hbm, tgt_hbm, gp_hbm, dr_hbm, m_hbm, v_hbm, om_hbm, new_global, new_momentum,
    tok, tokt, w, tgt, gp, dr, mo, ve, om,
    r_b1, r_b2, r_b3, r_b4, r_d1, r_d2, delta, r_c, r_x, r_z, avg,
    late_sum, late_x, late_f, late_avg,
    load_sem, part_sem, send_sems, recv_sems,
):
    rep = lax.axis_index("replica")
    me = lax.axis_index("fsdp")
    zh, x, c = rep // 8, (rep // 2) % 4, rep % 2
    y, zl = me // 2, me % 2
    yp, ym, y2 = (y + 1) % 4, (y + 3) % 4, (y + 2) % 4
    oz = 1 - zl

    def shard(a, b):
        return a * 2 + b

    to_yp, to_ym = (rep, shard(yp, zl)), (rep, shard(ym, zl))
    to_z = (rep, shard(y, oz))
    to_x = [(zh * 8 + ((x + k) % 4) * 2 + c, me) for k in range(4)]
    to_zh = ((1 - zh) * 8 + x * 2 + c, me)
    to_xc = [(zh * 8 + ((x + k) % 4) * 2 + (1 - c), me) for k in range(4)]
    friends = [to_yp, to_ym, to_z, to_zh] + to_x[1:] + to_xc
    links = Links(send_sems, recv_sems)
    ydirs = ((0, to_yp, ym, yp), (1, to_ym, yp, ym))

    parts = []
    for k in range(C):
        rows = pl.ds(k * R, R)
        a = pltpu.make_async_copy(gp_hbm.at[rows], gp.at[rows], part_sem.at[0, k])
        b = pltpu.make_async_copy(dr_hbm.at[0, rows], dr.at[rows], part_sem.at[1, k])
        a.start()
        b.start()
        parts.append((a, b))
    load_tok = pltpu.make_async_copy(tok_hbm.at[0], tok, load_sem.at[0])
    load_tgt = pltpu.make_async_copy(tgt_hbm.at[0], tgt, load_sem.at[1])
    load_m = pltpu.make_async_copy(m_hbm.at[0], mo, load_sem.at[2])
    load_v = pltpu.make_async_copy(v_hbm.at[0], ve, load_sem.at[3])
    load_om = pltpu.make_async_copy(om_hbm, om, load_sem.at[4])
    for copy in (load_tok, load_tgt, load_m, load_v, load_om):
        copy.start()

    barrier = pltpu.get_barrier_semaphore()
    for friend in friends:
        pl.semaphore_signal(barrier, inc=1, device_id=friend, device_id_type=MESH)

    def weights(k):
        for copy in parts[k]:
            copy.wait()
        rows = pl.ds(k * R, R)
        for h in range(2):
            cols = pl.ds(h * H, H)
            w[me, h, rows] = (gp[rows, cols] + dr[rows, cols]).astype(BF16)

    weights(0)
    pl.semaphore_wait(barrier, len(friends))

    def wpiece(s, k, part=None, h=None):
        rows = pl.ds(k * R, R) if part is None else pl.ds(k * R + (AP[0] if part else 0), AP[part])
        return w.at[s, :, rows] if h is None else w.at[s, h, rows]

    def wsend(name, piece, target):
        links.send(0, name, piece, piece, target)

    for k in range(C):
        if k:
            weights(k)
        for h, target, _, _ in ydirs:
            wsend(("a1", h, k), wpiece(me, k), target)
        wsend(("za", k), wpiece(me, k), to_z)

    load_tok.wait()
    keys = delta.at[:, pl.ds(0, TOK)]

    def dot_keys(s, k):
        cols = pl.ds(pl.multiple_of(s * ROWS + k * R, R), R)
        for h in range(2):
            keys[h] += jnp.dot(tok[:, cols], w[s, h, pl.ds(k * R, R)], preferred_element_type=F32)

    own_cols = pl.ds(pl.multiple_of(me * ROWS, ROWS), ROWS)
    for h in range(2):
        keys[h] = jnp.dot(tok[:, own_cols], w[me, h], preferred_element_type=F32)

    @pl.loop(0, D // 256)
    def _(b):
        at = pl.ds(pl.multiple_of(b * 256, 256), 256)
        tokt[at, :] = tok[:, at].T

    for k in range(C):
        links.recv(("za", k), wpiece(shard(y, oz), k))
        for h, target, _, _ in ydirs:
            wsend(("a2", h, k), wpiece(shard(y, oz), k, 0), target)
        for h, target, src, _ in ydirs:
            links.recv(("a1", h, k), wpiece(shard(src, zl), k))
            wsend(("a3", h, k), wpiece(shard(src, zl), k, None, h), target)
            wsend(("z3", k), wpiece(shard(src, zl), k, 1), to_z)
        dot_keys(shard(y, oz), k)
        dot_keys(shard(ym, zl), k)
        dot_keys(shard(yp, zl), k)
    for k in range(C):
        for h, target, src, _ in ydirs:
            links.recv(("a3", h, k), wpiece(shard(y2, zl), k, None, h))
            wsend(("z5", k), wpiece(shard(y2, zl), k, 1, h), to_z)
        for h, target, src, _ in ydirs:
            links.recv(("a2", h, k), wpiece(shard(src, oz), k, 0))
            wsend(("a4", k), wpiece(shard(src, oz), k, 0, h), target)
        dot_keys(shard(y2, zl), k)
    for k in range(C):
        links.recv(("z3", k), w.at[pl.ds(0, 2), :, pl.ds(0, AP[1])])
        dot_keys(shard(ym, oz), k)
        dot_keys(shard(yp, oz), k)
        links.recv(("z5", k), wpiece(shard(y2, oz), k, 1))
        links.recv(("a4", k), wpiece(shard(y2, oz), k, 0))
        dot_keys(shard(y2, oz), k)

    load_tgt.wait()
    for h in range(2):
        cols = pl.ds(h * H, H)
        tgt[:, cols] = (keys[h] - tgt[:, cols].astype(F32)).astype(BF16)

    links.sent(0, w.at[pl.ds(0, NS - 1)])
    g = w

    def grads(s, k):
        at = pl.ds(pl.multiple_of(s * ROWS + START[k], 16), SIZE[k])
        for h in range(2):
            g[s, h, pl.ds(START[k], SIZE[k])] = jnp.dot(
                tokt[at, :], tgt[:, pl.ds(h * H, H)], preferred_element_type=F32
            ).astype(BF16)

    def grows(k, part):
        return pl.ds(START[k] + (GROUPS[k][0] if part else 0), GROUPS[k][part])

    def gpiece(s, k, part, h=None):
        return g.at[s, :, grows(k, part)] if h is None else g.at[s, h, grows(k, part)]

    def gpair(a, k, h=None):
        two = pl.ds(pl.multiple_of(a * 2, 2), 2)
        return g.at[two, :, grows(k, 0)] if h is None else g.at[two, h, grows(k, 0)]

    def part_rows(k, part):
        return pl.ds(PSTART[part][k], GROUPS[k][part])

    def s1a(k):
        for z in range(2):
            grads(shard(y2, z), k)
        for h, target, _, _ in ydirs:
            links.send(1, ("b1", h, k), gpair(y2, k, h), r_b1.at[h, :, part_rows(k, 0)], target)
        links.send(1, ("da", k), gpiece(shard(y2, oz), k, 1), r_d1.at[3, :, part_rows(k, 1)], to_z)

    def s1b(k):
        @pl.loop(0, 2)
        def _(z):
            for a in (yp, ym, y):
                grads(shard(a, z), k)

        for j, a in ((0, yp), (1, ym), (2, y)):
            links.send(1, ("db", k), gpiece(shard(a, oz), k, 1), r_d1.at[j, :, part_rows(k, 1)], to_z)

    def s2y(h, k):
        p = part_rows(k, 0)
        _, target, _, dst = ydirs[h]
        links.recv(("b1", h, k), r_b1.at[h, :, p])
        own = gpair(dst, k, h)
        own[...] += r_b1[h, :, p]
        links.send(1, ("b2", k), gpair(dst, k), r_b2.at[h, :, :, p], target)

    def s2z(k):
        p = part_rows(k, 1)
        links.recv(("da", k), r_d1.at[3, :, p])
        own = gpiece(shard(y2, zl), k, 1)
        own[...] += r_d1[3, :, p]
        for h, target, _, _ in ydirs:
            links.send(1, ("b3", h, k), gpiece(shard(y2, zl), k, 1, h), r_b3.at[h, p], target)

    have_db = set()

    def s3y(h, k):
        p = part_rows(k, 1)
        _, target, _, dst = ydirs[h]
        if k not in have_db:
            have_db.add(k)
            links.recv(("db", k), r_d1.at[pl.ds(0, 3), :, p])
        links.recv(("b3", h, k), r_b3.at[h, p])
        one = gpiece(shard(dst, zl), k, 1, h)
        one[...] += r_d1[h, h, p] + r_b3[h, p]
        two = gpiece(shard(dst, zl), k, 1, 1 - h)
        two[...] += r_d1[h, 1 - h, p]
        links.send(1, ("b4", k), gpiece(shard(dst, zl), k, 1), r_b4.at[h, :, p], target)

    def s3z(k):
        p = part_rows(k, 0)
        links.recv(("b2", k), r_b2.at[:, :, :, p])
        own = gpiece(shard(y, oz), k, 0)
        own[...] += r_b2[0, oz, :, p] + r_b2[1, oz, :, p]
        links.send(1, ("d2", k), own, r_d2.at[:, p], to_z)

    def update(rows, cols, grad_sum):
        grad = grad_sum * (1.0 / (TOK * NS))
        glob = gp[rows, cols]
        local = glob + dr[rows, cols]
        moment = 0.9 * mo[rows, cols] + 0.1 * grad
        second = 0.95 * ve[rows, cols] + 0.05 * grad * grad
        step = moment / corr_one / (jnp.sqrt(second / corr_two) + 1e-08) + 0.1 * local
        return glob - (local - 0.003 * step)

    def updates(k, part, total):
        sub = next(b for b in (48, 32, 16) if GROUPS[k][part] % b == 0)

        @pl.loop(0, GROUPS[k][part] // sub)
        def _(i):
            off = pl.multiple_of(i * sub, 16)
            rows = pl.ds(START[k] + (GROUPS[k][0] if part else 0) + off, sub)
            p = pl.ds(PSTART[part][k] + off, sub)
            for h in range(2):
                delta[h, rows] = update(rows, pl.ds(h * H, H), total(h, rows, p))

    def s4(k):
        if k == 0:
            load_m.wait()
            load_v.wait()
        links.recv(("d2", k), r_d2.at[:, part_rows(k, 0)])
        updates(
            k, 0,
            lambda h, rows, p: (g[me, h, rows].astype(F32) + r_d2[h, p].astype(F32))
            + (r_b2[0, zl, h, p].astype(F32) + r_b2[1, zl, h, p].astype(F32)),
        )
        links.recv(("b4", k), r_b4.at[:, :, part_rows(k, 1)])
        updates(
            k, 1,
            lambda h, rows, p: (g[me, h, rows].astype(F32) + r_d1[2, h, p].astype(F32))
            + (r_b4[0, h, p].astype(F32) + r_b4[1, h, p].astype(F32)),
        )
        if k < N - FAST:
            rows = pl.ds(START[k], SIZE[k])
            links.send(2, ("c", k), delta.at[1 - c, rows], r_c.at[rows], to_xc[0])
        else:
            rows = pl.ds(START[k], SIZE[k])
            late_sum[:, pl.ds(START[k] - LATE, SIZE[k])] = delta[:, rows].astype(BF16)
            for j, other, target in others():
                half = 1 - c if other else c
                links.send(
                    2, ("x", k), late_sum.at[half, late_rows(k, (x + j) % 4)], f_slot(j, other, k), target
                )

    def others():
        found = [(j, 0, to_x[j]) for j in (2, 1, 3)] + [(j, 1, to_xc[j]) for j in (2, 1, 3, 0)]
        return sorted(found, key=lambda f: (2, 1, 3, 0).index(f[0]))

    def x_rows(k, a):
        q = SIZE[k] // 4
        return pl.ds(pl.multiple_of(START[k] + a * q, 8), q)

    def late_rows(k, a):
        q = SIZE[k] // 4
        return pl.ds(pl.multiple_of(START[k] - LATE + a * q, 16), q)

    def q_rows(k):
        return pl.ds(START[k] // 4, SIZE[k] // 4)

    def x_slots(k):
        if k < WIDE:
            return r_x.at[:, q_rows(k)]
        return late_x.at[:, pl.ds((START[k] - LATE) // 4, SIZE[k] // 4)]

    def f_slot(j, other, k):
        q = SIZE[k] // 4
        return late_f.at[j * 2 + other, pl.ds((START[k] - START[N - FAST]) // 4, q)]

    def f_slots(k):
        q = SIZE[k] // 4
        return late_f.at[pl.ds(1, 7), pl.ds((START[k] - START[N - FAST]) // 4, q)]

    def s5(k):
        rows = pl.ds(START[k], SIZE[k])
        links.recv(("c", k), r_c.at[rows])
        delta[c, rows] += r_c[rows]
        if k >= WIDE:
            late_sum[c, pl.ds(START[k] - LATE, SIZE[k])] = delta[c, rows].astype(BF16)
        for j in (2, 1, 3):
            at = (x + j) % 4
            piece = delta.at[c, x_rows(k, at)] if k < WIDE else late_sum.at[c, late_rows(k, at)]
            links.send(2, ("x", k), piece, x_slots(k).at[j - 1], to_x[j])

    def s6(k):
        at = x_rows(k, x)
        if k < N - FAST:
            got = x_slots(k)
            links.recv(("x", k), got)
            delta[c, at] += got[0].astype(F32) + got[1].astype(F32) + got[2].astype(F32)
        else:
            links.recv(("x", k), f_slots(k))
            total = delta[c, at]
            for j, other, _ in others():
                total += f_slot(j, other, k)[...].astype(F32)
            delta[c, at] = total
        links.send(2, ("zh", k), delta.at[c, at], r_z.at[q_rows(k)], to_zh)

    def s7(k):
        links.recv(("zh", k), r_z.at[q_rows(k)])
        at = x_rows(k, x)
        average = (delta[c, at] + r_z[q_rows(k)]) * (1.0 / REPLICAS)
        if k < WIDE:
            piece = avg.at[c, at]
            piece[...] = average
        else:
            piece = late_avg.at[c, late_rows(k, x)]
            piece[...] = average.astype(BF16)
        if k < N - FAST:
            for j in (2, 1, 3):
                links.send(2, ("xg", k), piece, piece, to_x[j])
        else:
            for j, other, target in others():
                links.send(2, ("xg", k), piece, piece, target)

    def averages(half, k):
        if k < WIDE:
            return avg.at[half, pl.ds(START[k], SIZE[k])]
        return late_avg.at[half, pl.ds(START[k] - LATE, SIZE[k])]

    def outer(k, half):
        sub = 32

        @pl.loop(0, SIZE[k] // sub)
        def _(i):
            off = pl.multiple_of(i * sub, sub)
            rows = pl.ds(START[k] + off, sub)
            cols = pl.ds(pl.multiple_of(half * H, H), H)
            average = averages(half, k)[pl.ds(off, sub)].astype(F32)
            momentum_next = 0.9 * om[rows, cols] + average
            new_momentum[rows, cols] = momentum_next
            new_global[rows, cols] = gp[rows, cols] - 0.7 * (0.9 * momentum_next + average)

    def s8(k):
        links.recv(("xg", k), x_slots(k))
        links.send(2, ("cg", k), averages(c, k), averages(c, k), to_xc[0])
        if k == 0:
            load_om.wait()
        outer(k, c)

    def s9(k):
        if k < N - FAST:
            links.recv(("cg", k), averages(1 - c, k))
            outer(k, 1 - c)
        else:
            links.recv(("xg", k), f_slots(k))
            outer(k, 0)
            outer(k, 1)

    s2y0, s2y1 = functools.partial(s2y, 0), functools.partial(s2y, 1)
    s3y0, s3y1 = functools.partial(s3y, 0), functools.partial(s3y, 1)
    order = (
        (s1a, 4), (s1a, 0), (s1b, 0), (s1a, 2), (s2z, 0), (s1a, 1), (s1a, 3), (s2y1, 0), (s2y0, 0), (s1b, 1),
        (s2y0, 1), (s1b, 2), (s2y1, 1), (s3z, 0), (s2z, 1), (s3y1, 0), (s2y1, 2), (s3y0, 0), (s3z, 1),
        (s2y0, 2), (s3y0, 1), (s1b, 4), (s1b, 3), (s2y0, 3), (s3y1, 1), (s4, 0), (s2z, 2), (s2y1, 3), (s5, 0),
        (s3z, 2), (s4, 1), (s2z, 3), (s1a, 5), (s3y1, 2), (s2y0, 4), (s6, 0), (s3y0, 2), (s2y1, 4), (s3z, 3),
        (s5, 1), (s2z, 4), (s3y1, 3), (s3y0, 3), (s2z, 5), (s1b, 5), (s2y0, 5), (s7, 0), (s2y1, 5), (s4, 2),
        (s3y0, 4), (s3z, 4), (s3y1, 4), (s6, 1), (s4, 3), (s5, 2), (s3y1, 5), (s3y0, 5), (s3z, 5), (s4, 4),
        (s5, 3), (s5, 4), (s6, 2), (s4, 5), (s8, 0), (s7, 1), (s6, 3), (s6, 4), (s6, 5), (s7, 2), (s7, 3),
        (s8, 1), (s7, 4), (s7, 5), (s9, 0), (s8, 2), (s9, 1), (s8, 3), (s8, 4), (s9, 2), (s9, 5), (s9, 3),
        (s9, 4),
    )
    for stage, k in order:
        stage(k)
    links.sent(1, tokt.at[pl.ds(0, (NS - 1) * ROWS)])
    links.sent(2, tokt.at[pl.ds(0, AVERAGE_KIB)])


def step(*arrays):
    in_hbm = pl.BlockSpec(memory_space=pltpu.HBM)
    in_vmem = pl.BlockSpec(memory_space=pltpu.VMEM)
    p1, p2 = PROWS
    return pl.pallas_call(
        kernel,
        out_shape=(jax.ShapeDtypeStruct((ROWS, KV), F32),) * 2,
        in_specs=[in_hbm] * 7,
        out_specs=(in_vmem, in_vmem),
        scratch_shapes=[
            pltpu.VMEM((TOK, D), BF16),
            pltpu.VMEM((D, TOK), BF16),
            pltpu.VMEM((NS, 2, ROWS, H), BF16),
            pltpu.VMEM((TOK, KV), BF16),
            pltpu.VMEM((ROWS, KV), F32),
            pltpu.VMEM((ROWS, KV), F32),
            pltpu.VMEM((ROWS, KV), F32),
            pltpu.VMEM((ROWS, KV), F32),
            pltpu.VMEM((ROWS, KV), F32),
            pltpu.VMEM((2, 2, p1, H), BF16),
            pltpu.VMEM((2, 2, 2, p1, H), BF16),
            pltpu.VMEM((2, p2, H), BF16),
            pltpu.VMEM((2, 2, p2, H), BF16),
            pltpu.VMEM((4, 2, p2, H), BF16),
            pltpu.VMEM((2, p1, H), BF16),
            pltpu.VMEM((2, ROWS, H), F32),
            pltpu.VMEM((ROWS, H), F32),
            pltpu.VMEM((3, LATE // 4, H), F32),
            pltpu.VMEM((ROWS // 4, H), F32),
            pltpu.VMEM((2, LATE, H), F32),
            pltpu.VMEM((2, ROWS - LATE, H), BF16),
            pltpu.VMEM((3, (ROWS - LATE) // 4, H), BF16),
            pltpu.VMEM((8, sum(SIZE[N - FAST :]) // 4, H), BF16),
            pltpu.VMEM((2, ROWS - LATE, H), BF16),
            pltpu.SemaphoreType.DMA((5,)),
            pltpu.SemaphoreType.DMA((2, C)),
            pltpu.SemaphoreType.DMA((3,)),
            pltpu.SemaphoreType.DMA((N_MESSAGES,)),
        ],
        compiler_params=pltpu.CompilerParams(
            collective_id=0, has_side_effects=True, vmem_limit_bytes=VMEM_KIB * 2**10
        ),
        cost_estimate=pl.CostEstimate(
            flops=4 * TOK * D * KV, bytes_accessed=24 * 2**20, transcendentals=ROWS * KV
        ),
        name="inner_and_outer_step",
    )(*(pltpu.with_memory_space_constraint(a, pltpu.HBM) for a in arrays))


def write_kernel(a_ref, b_ref, a_hbm, b_hbm, sems):
    copies = []
    for i, (src, dst) in enumerate(((a_ref, a_hbm), (b_ref, b_hbm))):
        for q in range(2):
            rows = pl.ds(q * ROWS // 2, ROWS // 2)
            copies.append(pltpu.make_async_copy(src.at[rows], dst.at[rows], sems.at[i, q]))
    for copy in copies:
        copy.start()
    for copy in copies:
        copy.wait()


def whole(*arrays):
    return pl.pallas_call(
        write_kernel,
        out_shape=(jax.ShapeDtypeStruct((ROWS, KV), F32),) * 2,
        in_specs=[pl.BlockSpec(memory_space=pl.ANY)] * 2,
        out_specs=(pl.BlockSpec(memory_space=pltpu.HBM),) * 2,
        scratch_shapes=[pltpu.SemaphoreType.DMA((2, 2))],
        compiler_params=pltpu.CompilerParams(vmem_limit_bytes=2**20),
        name="write_results",
    )(*step(*arrays))


def solution(mesh):
    in_specs = (
        P("replica", "fsdp", None),
        P("replica", "fsdp", None),
        P("fsdp", None),
        P("replica", "fsdp", None),
        P("replica", "fsdp", None),
        P("replica", "fsdp", None),
        P("fsdp", None),
    )
    out_specs = (P("fsdp", None), P("fsdp", None))
    return jax.shard_map(whole, mesh=mesh, in_specs=in_specs, out_specs=out_specs, check_vma=False)
```
